512 devices in a mesh: seq: 64 (over z, y), chan: 8 (over x, core).
Axes of the slice: x: 4, y: 8, z: 8, core: 2. Of those that a mesh axis runs over, the one named last changes fastest.
Arguments:
- d_out: bfloat16 [12288, 4096], P('seq', 'chan'), may hold values from -6 to 6
- x_branch: bfloat16 [12288, 4096], P('seq', 'chan'), may hold values from -6 to 6
- gate_branch: bfloat16 [12288, 4096], P('seq', 'chan'), may hold values from -5 to 5
- recurrence_gate: bfloat16 [12288, 4096], P('seq', 'chan'), may hold values from -6 to 6
- input_gate: bfloat16 [12288, 4096], P('seq', 'chan'), may hold values from -6 to 6
- conv_weight: float32 [4, 4096], P(None, 'chan'), may hold values from -3 to 3
- conv_bias: float32 [4096], P('chan'), may hold values from -3 to 3
- decay_level: int32 [4096], P('chan'), may hold values from 0 to 15
- w_in: bfloat16 [4096, 4096], P(('chan', 'seq')), may hold values from -0.09375 to 0.09375
- w_out: bfloat16 [4096, 4096], P(('chan', 'seq')), may hold values from -0.09375 to 0.09375
Outputs:
- d_input: bfloat16 [12288, 4096], P('seq', 'chan')
- d_gate: bfloat16 [12288, 4096], P('seq', 'chan')
- d_recurrence_gate: bfloat16 [12288, 4096], P('seq', 'chan')
- d_input_gate: bfloat16 [12288, 4096], P('seq', 'chan')
The draws below stay inside these ranges and needn't reach their ends.
All inputs are finite; a program needn't handle non-finite values.
Results may differ from the reference program's by a relative error of at most 0.017.
Values may be sent and summed in bfloat16 or wider, within the bound.
No kernel may reach another device: no remote copies, remote signals or barrier semaphores. Data moves between devices by JAX's collectives and lax.ppermute only.
A program may use at most 64 MiB of HBM per device.

```python
import jax
import jax.numpy as jnp
from jax import lax

D = 4096
R = 4096
TOK_DEV = 192
LEVELS = 16
LENGTH = 12288
N_CHAN = 8


def draw_recurrence_gate(key, part):
    key = jax.random.fold_in(key, 11)
    noise_key, chan_key, block_key = jax.random.split(key, 3)
    blocks = LENGTH // TOK_DEV
    base = 2.0 * jax.random.normal(noise_key, (blocks, TOK_DEV, R), jnp.float32)
    chan_shift = jax.random.uniform(chan_key, (1, 1, R), jnp.float32, -4.0, 4.0)
    block_shift = jax.random.uniform(block_key, (blocks, 1, 1), jnp.float32, -2.0, 2.0)
    values = jnp.clip(base + chan_shift + block_shift, -6.0, 6.0).reshape(LENGTH, R)
    return values.astype(jnp.bfloat16)


def with_ends(entries, key, low, largest):
    extent = entries.shape
    index_at = [jax.random.randint(jax.random.fold_in(key, axis), (), 0, extent[axis]) for axis in range(len(extent))]
    entries = entries.at[tuple(index_at)].set(low)
    longest = extent.index(max(extent))
    index_at[longest] = (index_at[longest] + 1) % extent[longest]
    return entries.at[tuple(index_at)].set(largest)


def level_of(rng, extent, pieces, low, top_value):
    gain, own = 1.0, jax.random.fold_in(rng, 6)
    for axis_at, shards_of in pieces:
        steps = jnp.exp(jax.random.uniform(jax.random.fold_in(own, axis_at), (shards_of,), jnp.float32, low / len(pieces), top_value / len(pieces)))
        gain = gain * jnp.repeat(steps, extent[axis_at] // shards_of).reshape([-1 if axis == axis_at else 1 for axis in range(len(extent))])
    return gain


def bell_draw(key, dims, scale, most, pieces=(), dtype=jnp.bfloat16):
    factor_of = level_of(key, dims, pieces, -0.22, 0.18) if pieces else 1.0
    drawn = jax.random.normal(key, dims, jnp.float32) * scale * factor_of
    return jnp.minimum(jnp.maximum(drawn, -most), most).astype(dtype)


def setup_inputs(seed: int = 0) -> dict:
    seeds = jax.random.split(jax.random.key(seed), 11)
    d_out = bell_draw(seeds[0], (LENGTH, D), 1.0, 6.0, ((0, 64), (1, 8)))
    x_branch = bell_draw(seeds[1], (LENGTH, R), 1.0, 6.0, ((0, 64), (1, 8)))
    gate_branch = bell_draw(seeds[2], (LENGTH, R), 1.0, 5.0, ((0, 64), (1, 8)))
    recurrence_gate = draw_recurrence_gate(jax.random.fold_in(seeds[10], 71), 0)
    input_gate = bell_draw(seeds[4], (LENGTH, R), 1.5, 6.0, ((0, 64), (1, 8)))
    conv_weight = bell_draw(seeds[5], (4, R), 0.6, 3.0, ((1, 8),), jnp.float32)
    conv_bias = bell_draw(seeds[6], (R,), 0.7, 3.0, ((0, 8),), jnp.float32)
    decay_level = with_ends(jax.random.randint(seeds[7], (R,), 0, LEVELS), jax.random.fold_in(seeds[7], 1), 0, LEVELS - 1).astype(jnp.int32)
    w_in = bell_draw(seeds[8], (D, R), D ** -0.5, 0.09375, ((0, 512),))
    w_out = bell_draw(seeds[9], (R, D), R ** -0.5, 0.09375, ((0, 512),))
    return {"d_out": d_out, "x_branch": x_branch, "gate_branch": gate_branch, "recurrence_gate": recurrence_gate, "input_gate": input_gate, "conv_weight": conv_weight, "conv_bias": conv_bias, "decay_level": decay_level, "w_in": w_in, "w_out": w_out}


def decay_table(length):
    levels = jnp.arange(LEVELS).astype(jnp.float32)
    half = LEVELS // 2
    slow_rates = 0.25 * jnp.power(16.0, levels / (half - 1.0)) / (8.0 * length)
    fast_rates = jnp.power(4.0, (levels - half) / (half - 1.0)) / 640.0
    return -jnp.where(levels < half, slow_rates, fast_rates)

def combine_affine(earlier, later):
    return (earlier[0] * later[0], later[0] * earlier[1] + later[1])

def gelu_parts(gate):
    normal_cdf = 0.5 * (1.0 + lax.erf(gate * 0.7071067811865476))
    density = jnp.exp(-0.5 * gate * gate) * 0.3989422804014327
    return (gate * normal_cdf, normal_cdf + gate * density)

def reference(d_out, x_branch, gate_branch, recurrence_gate, input_gate, conv_weight, conv_bias, decay_level, w_in, w_out):
    log_table = decay_table(LENGTH)
    block_width = R // N_CHAN
    gate_grads = []
    recur_grads = []
    input_grads = []
    input_total = jnp.zeros((LENGTH, D), jnp.float32)
    for block_index in range(N_CHAN):
        low = block_index * block_width
        high = low + block_width
        log_decay = log_table[decay_level[low:high]]
        branch = x_branch[:, low:high].astype(jnp.float32)
        padded = jnp.concatenate([jnp.zeros((3, block_width), jnp.float32), branch], axis=0)
        conv_out = conv_bias[low:high] + sum((conv_weight[offset, low:high] * padded[3 - offset:3 - offset + LENGTH] for offset in range(4)))
        recur = jax.nn.sigmoid(recurrence_gate[:, low:high].astype(jnp.float32))
        inward = jax.nn.sigmoid(input_gate[:, low:high].astype(jnp.float32))
        log_step = 8.0 * recur * log_decay
        decay = jnp.exp(log_step)
        beta = jnp.sqrt(-jnp.expm1(2.0 * log_step))
        gated_in = inward * conv_out
        states = lax.associative_scan(combine_affine, (decay, beta * gated_in), axis=0)[1]
        d_lru = jnp.dot(d_out, w_out[low:high, :].T, preferred_element_type=jnp.float32)
        gelu_gate, gelu_slope = gelu_parts(gate_branch[:, low:high].astype(jnp.float32))
        d_direct = d_lru * gelu_gate
        gate_grads.append((d_lru * states * gelu_slope).astype(jnp.bfloat16))
        kappa = lax.associative_scan(combine_affine, (decay, decay * d_direct), axis=0, reverse=True)[1]
        zero_row = jnp.zeros((1, block_width), jnp.float32)
        adjoint = d_direct + jnp.concatenate([kappa[1:], zero_row], axis=0)
        states_prev = jnp.concatenate([zero_row, states[:-1]], axis=0)
        d_step = adjoint * (decay * states_prev - gated_in * decay * decay / beta)
        recur_grads.append((d_step * 8.0 * log_decay * recur * (1.0 - recur)).astype(jnp.bfloat16))
        d_gated = adjoint * beta
        input_grads.append((d_gated * conv_out * inward * (1.0 - inward)).astype(jnp.bfloat16))
        d_conv = d_gated * inward
        padded_after = jnp.concatenate([d_conv, jnp.zeros((3, block_width), jnp.float32)], axis=0)
        d_branch = sum((conv_weight[offset, low:high] * padded_after[offset:offset + LENGTH] for offset in range(4))).astype(jnp.bfloat16)
        partial_term = jnp.dot(d_branch, w_in[:, low:high].T, preferred_element_type=jnp.float32).astype(jnp.bfloat16)
        partial_term = lax.optimization_barrier(partial_term)
        input_total = input_total + partial_term.astype(jnp.float32)
    d_input = input_total.astype(jnp.bfloat16)
    return (d_input, jnp.concatenate(gate_grads, axis=1), jnp.concatenate(recur_grads, axis=1), jnp.concatenate(input_grads, axis=1))
```

```python
import jax
import jax.numpy as jnp
from jax import lax
from jax.experimental import pallas as pl
from jax.experimental.pallas import tpu as pltpu
from jax.sharding import Mesh, PartitionSpec as P

LEVELS = 16
SEQ = ("z", "y")
CHAN = ("x", "k")
SUB = 8
F32 = jnp.float32
BF16 = jnp.bfloat16
VMEM_LIMIT = 48 * 1024 * 1024


def decay_table(length):
    levels = jnp.arange(LEVELS).astype(F32)
    half = LEVELS // 2
    slow_rates = 0.25 * jnp.power(16.0, levels / (half - 1.0)) / (8.0 * length)
    fast_rates = jnp.power(4.0, (levels - half) / (half - 1.0)) / 640.0
    return -jnp.where(levels < half, slow_rates, fast_rates)


def gelu_parts(gate):
    normal_cdf = 0.5 * (1.0 + lax.erf(gate * 0.7071067811865476))
    density = jnp.exp(-0.5 * gate * gate) * 0.3989422804014327
    return (gate * normal_cdf, normal_cdf + gate * density)


def sigmoid(value):
    return 1.0 / (1.0 + jnp.exp(-value))


def expm1(value):
    series = jnp.ones_like(value)
    for term in range(9, 1, -1):
        series = 1.0 + value * (1.0 / term) * series
    return jnp.where(jnp.abs(value) < 0.5, value * series, jnp.exp(value) - 1.0)


def local_scan(a, b, reverse, a_out, b_out):
    rows, width = a.shape
    tiles = rows // SUB
    a = a.reshape(tiles, SUB, width)
    b = b.reshape(tiles, SUB, width)
    row = lax.broadcasted_iota(jnp.int32, a.shape, 1)
    for step in (1, 2, 4):
        shift = SUB - step if reverse else step
        inside = row < SUB - step if reverse else row >= step
        a_from = jnp.where(inside, pltpu.roll(a, shift, 1), 1.0)
        b_from = jnp.where(inside, pltpu.roll(b, shift, 1), 0.0)
        b = b + a * b_from
        a = a * a_from
    prod = jnp.ones((1, width), F32)
    state = jnp.zeros((1, width), F32)
    edge = 0 if reverse else SUB - 1
    for tile in reversed(range(tiles)) if reverse else range(tiles):
        here_b = b[tile] + a[tile] * state
        here_a = a[tile] * prod
        b_out[pl.ds(tile * SUB, SUB), :] = here_b
        a_out[pl.ds(tile * SUB, SUB), :] = here_a
        state = here_b[edge : edge + 1]
        prod = here_a[edge : edge + 1]
    return prod, state


def shift_up(value, last):
    rows = value.shape[0]
    row = lax.broadcasted_iota(jnp.int32, value.shape, 0)
    return jnp.where(row == rows - 1, last, pltpu.roll(value, rows - 1, 0))


def before_kernel(
    x_ref, prev_ref, rec_ref, inw_ref, cw_ref, cb_ref, ld_ref,
    decay_ref, beta_ref, conv_ref, cum_ref, local_ref, post_ref, ends_ref, front_ref,
    padded, scan_a, scan_b,
):
    rows = x_ref.shape[0]
    lead = prev_ref.shape[0]
    padded[pl.ds(0, lead), :] = prev_ref[...].astype(F32)
    padded[pl.ds(lead, rows), :] = x_ref[...].astype(F32)
    conv = jnp.zeros(x_ref.shape, F32)
    for lag in range(4):
        conv = conv + cw_ref[lag : lag + 1, :] * padded[pl.ds(lead - lag, rows), :]
    conv = cb_ref[...] + conv
    recur = sigmoid(rec_ref[...].astype(F32))
    inward = sigmoid(inw_ref[...].astype(F32))
    log_step = 8.0 * recur * ld_ref[...]
    decay = jnp.exp(log_step)
    beta = jnp.sqrt(-expm1(2.0 * log_step))
    decay_ref[...] = decay
    beta_ref[...] = beta
    conv_ref[...] = conv
    prod, state = local_scan(decay, beta * (inward * conv), False, cum_ref, local_ref)
    ends_ref[...] = jnp.concatenate([prod, state], axis=0)
    local_scan(decay, jnp.zeros_like(decay), True, scan_a, scan_b)
    post = shift_up(scan_a[...], 1.0)
    post_ref[...] = post
    front_ref[...] = (post * beta * inward)[:SUB]


def before(x_branch, prev, recurrence_gate, input_gate, conv_weight, conv_bias, log_decay):
    rows, width = x_branch.shape
    full = jax.ShapeDtypeStruct((rows, width), F32)
    return pl.pallas_call(
        before_kernel,
        out_shape=(full,) * 6
        + (jax.ShapeDtypeStruct((2, width), F32), jax.ShapeDtypeStruct((SUB, width), F32)),
        scratch_shapes=[
            pltpu.VMEM((rows + prev.shape[0], width), F32),
            pltpu.VMEM((rows, width), F32),
            pltpu.VMEM((rows, width), F32),
        ],
        compiler_params=pltpu.CompilerParams(vmem_limit_bytes=VMEM_LIMIT),
    )(x_branch, prev, recurrence_gate, input_gate, conv_weight, conv_bias, log_decay)


def adjoint_kernel(
    core_ref, own_ref, other_ref, w_ref, gate_ref, decay_ref, beta_ref, inw_ref, ends_ref,
    dlru_ref, adj_ref, front_ref, carry_ref,
    acc, scan_a, scan_b,
):
    step = pl.program_id(0)
    half = w_ref.shape[1] // 2

    @pl.when(step == 0)
    def _():
        acc[...] = jnp.zeros_like(acc)

    def add(first, second):
        dims = (((1,), (1,)), ((), ()))
        acc[...] += lax.dot_general(
            first[0], w_ref[:, :half], dims, preferred_element_type=F32
        ) + lax.dot_general(second[0], w_ref[:, half:], dims, preferred_element_type=F32)

    @pl.when(core_ref[0] == 0)
    def _():
        add(own_ref[...], other_ref[...])

    @pl.when(core_ref[0] != 0)
    def _():
        add(other_ref[...], own_ref[...])

    @pl.when(step == pl.num_programs(0) - 1)
    def _():
        d_lru = acc[...]
        dlru_ref[...] = d_lru
        d_direct = d_lru * gelu_parts(gate_ref[...].astype(F32))[0]
        decay = decay_ref[...]
        _, first = local_scan(decay, decay * d_direct, True, scan_a, scan_b)
        adj = d_direct + shift_up(scan_b[...], 0.0)
        adj_ref[...] = adj
        inward = sigmoid(inw_ref[:16, :].astype(F32))[:SUB]
        front_ref[...] = adj[:SUB] * beta_ref[:SUB, :] * inward
        mine = jnp.concatenate([ends_ref[...], first], axis=0)
        carry_ref[...] = jnp.broadcast_to(mine[None], carry_ref.shape)


def adjoint(core, own, other, weights, gate, decay, beta, input_gate, ends, seq_count):
    rows, width = gate.shape
    steps = own.shape[0]
    full = jax.ShapeDtypeStruct((rows, width), F32)
    whole = lambda shape: pl.BlockSpec(shape, lambda i: (0,) * len(shape))
    return pl.pallas_call(
        adjoint_kernel,
        grid=(steps,),
        in_specs=[
            pl.BlockSpec(memory_space=pltpu.SMEM),
            pl.BlockSpec((1, rows, width), lambda i: (i, 0, 0)),
            pl.BlockSpec((1, rows, width), lambda i: (i, 0, 0)),
            pl.BlockSpec((width, 2 * width), lambda i: (0, i)),
            whole((rows, width)),
            whole((rows, width)),
            whole((rows, width)),
            whole((rows, width)),
            whole((2, width)),
        ],
        out_specs=[
            whole((rows, width)),
            whole((rows, width)),
            whole((SUB, width)),
            whole((seq_count, 3, width)),
        ],
        out_shape=(
            full,
            full,
            jax.ShapeDtypeStruct((SUB, width), F32),
            jax.ShapeDtypeStruct((seq_count, 3, width), F32),
        ),
        scratch_shapes=[pltpu.VMEM((rows, width), F32)] * 3,
        compiler_params=pltpu.CompilerParams(vmem_limit_bytes=VMEM_LIMIT),
    )(core, own, other, weights, gate, decay, beta, input_gate, ends)


def branch_kernel(
    place_ref, carry_ref, adj_ref, post_ref, beta_ref, inw_ref, cw_ref, front_a_ref, front_b_ref,
    branch_ref, adjoint_ref, state_ref,
    padded,
):
    rows, width = adj_ref.shape
    place = place_ref[0]
    count = carry_ref.shape[0]
    state = jnp.zeros((1, width), F32)
    beyond = jnp.zeros((1, width), F32)
    kappa = jnp.zeros((1, width), F32)
    for i in range(count - 1):
        state = jnp.where(i < place, carry_ref[i, 1:2] + carry_ref[i, 0:1] * state, state)
    for i in reversed(range(1, count)):
        here = carry_ref[i, 2:3] + carry_ref[i, 0:1] * kappa
        beyond = jnp.where(i == place + 1, kappa, beyond)
        kappa = jnp.where(i > place, here, kappa)
    adj = adj_ref[...] + post_ref[...] * kappa
    d_conv = adj * beta_ref[...] * sigmoid(inw_ref[...].astype(F32))
    padded[pl.ds(0, rows), :] = d_conv
    padded[pl.ds(rows, SUB), :] = front_a_ref[...] + front_b_ref[...] * beyond
    total = jnp.zeros((rows, width), F32)
    for lag in range(4):
        total = total + cw_ref[lag : lag + 1, :] * padded[pl.ds(lag, rows), :]
    branch_ref[...] = total.astype(BF16)
    adjoint_ref[...] = adj
    state_ref[...] = state


def branch(place, carry, adj, post, beta, input_gate, conv_weight, front_a, front_b):
    rows, width = adj.shape
    vmem = pl.BlockSpec(memory_space=pltpu.VMEM)
    return pl.pallas_call(
        branch_kernel,
        in_specs=[pl.BlockSpec(memory_space=pltpu.SMEM)] + [vmem] * 8,
        out_shape=(
            jax.ShapeDtypeStruct((rows, width), BF16),
            jax.ShapeDtypeStruct((rows, width), F32),
            jax.ShapeDtypeStruct((1, width), F32),
        ),
        scratch_shapes=[pltpu.VMEM((rows + SUB, width), F32)],
        compiler_params=pltpu.CompilerParams(vmem_limit_bytes=VMEM_LIMIT),
    )(place, carry, adj, post, beta, input_gate, conv_weight, front_a, front_b)


def gates_kernel(
    dlru_ref, adj_ref, state_ref, cum_ref, local_ref, decay_ref, beta_ref, conv_ref,
    gate_ref, rec_ref, inw_ref, ld_ref,
    dgate_ref, drec_ref, dinw_ref,
):
    carried = state_ref[...]
    states = local_ref[...] + cum_ref[...] * carried
    slope = gelu_parts(gate_ref[...].astype(F32))[1]
    dgate_ref[...] = (dlru_ref[...] * states * slope).astype(BF16)
    row = lax.broadcasted_iota(jnp.int32, states.shape, 0)
    states_prev = jnp.where(row == 0, carried, pltpu.roll(states, 1, 0))
    recur = sigmoid(rec_ref[...].astype(F32))
    inward = sigmoid(inw_ref[...].astype(F32))
    decay = decay_ref[...]
    beta = beta_ref[...]
    conv = conv_ref[...]
    adj = adj_ref[...]
    d_step = adj * (decay * states_prev - inward * conv * decay * decay / beta)
    drec_ref[...] = (d_step * 8.0 * ld_ref[...] * recur * (1.0 - recur)).astype(BF16)
    dinw_ref[...] = (adj * beta * conv * inward * (1.0 - inward)).astype(BF16)


def gates(*arrays):
    out = jax.ShapeDtypeStruct(arrays[0].shape, BF16)
    return pl.pallas_call(
        gates_kernel,
        out_shape=(out,) * 3,
        compiler_params=pltpu.CompilerParams(vmem_limit_bytes=VMEM_LIMIT),
    )(*arrays)


def input_kernel(rows_ref, w_ref, out_ref, acc):
    step = pl.program_id(0)
    half = w_ref.shape[1] // 2

    @pl.when(step == 0)
    def _():
        acc[...] = jnp.zeros_like(acc)

    dims = (((1,), (1,)), ((), ()))
    acc[...] += lax.dot_general(
        rows_ref[0], w_ref[:, :half], dims, preferred_element_type=F32
    ) + lax.dot_general(rows_ref[1], w_ref[:, half:], dims, preferred_element_type=F32)

    @pl.when(step == pl.num_programs(0) - 1)
    def _():
        out_ref[...] = acc[...].astype(BF16)


def input_grad(gathered, weights):
    count, rows, width = gathered.shape
    steps = count // 2
    return pl.pallas_call(
        input_kernel,
        grid=(steps,),
        in_specs=[
            pl.BlockSpec((2, rows, width), lambda i: (i, 0, 0)),
            pl.BlockSpec((width, 2 * width), lambda i: (0, steps + i)),
        ],
        out_specs=pl.BlockSpec((rows, width), lambda i: (0, 0)),
        out_shape=jax.ShapeDtypeStruct((rows, width), BF16),
        scratch_shapes=[pltpu.VMEM((rows, width), F32)],
        compiler_params=pltpu.CompilerParams(vmem_limit_bytes=VMEM_LIMIT),
    )(gathered, weights)


def shards(
    d_out,
    x_branch,
    gate_branch,
    recurrence_gate,
    input_gate,
    conv_weight,
    conv_bias,
    decay_level,
    w_in,
    w_out,
):
    tok_rows, chan_width = x_branch.shape
    seq_count = lax.axis_size(SEQ)
    place = lax.axis_index(SEQ).astype(jnp.int32).reshape(1)
    core = lax.axis_index("k").astype(jnp.int32).reshape(1)
    forward = [(i, i + 1) for i in range(seq_count - 1)]
    backward = [(i + 1, i) for i in range(seq_count - 1)]
    weights = lax.all_gather(jnp.concatenate([w_out, w_in], axis=1), SEQ, axis=0, tiled=True)
    prev = lax.ppermute(x_branch[tok_rows - 16 :], SEQ, forward)
    own = lax.all_gather(d_out, "x")
    other = lax.ppermute(own, "k", [(0, 1), (1, 0)])
    log_table = decay_table(tok_rows * seq_count)
    onehot = decay_level[:, None] == jnp.arange(LEVELS)[None, :]
    log_decay = jnp.sum(jnp.where(onehot, log_table[None, :], 0.0), axis=1)[None, :]
    decay, beta, conv_out, cum_decay, local_states, post, ends, front_b = before(
        x_branch, prev, recurrence_gate, input_gate, conv_weight, conv_bias[None, :], log_decay
    )
    next_b = lax.ppermute(front_b, SEQ, backward)
    d_lru, adj_local, front_a, carry = adjoint(
        core, own, other, weights, gate_branch, decay, beta, input_gate, ends, seq_count
    )
    next_a = lax.ppermute(front_a, SEQ, backward)
    carries = lax.all_to_all(carry, SEQ, 0, 0)
    d_branch, adj, state_in = branch(
        place, carries, adj_local, post, beta, input_gate, conv_weight, next_a, next_b
    )
    gathered = lax.all_gather(d_branch, CHAN)
    d_gate, d_recurrence_gate, d_input_gate = gates(
        d_lru, adj, state_in, cum_decay, local_states, decay, beta, conv_out,
        gate_branch, recurrence_gate, input_gate, log_decay,
    )
    d_input = input_grad(gathered, weights)
    return (d_input, d_gate, d_recurrence_gate, d_input_gate)


def solution(mesh):
    fine = Mesh(mesh.devices.reshape(8, 8, 4, 2), SEQ + CHAN)
    tokens = P(SEQ, CHAN)
    rows = P(CHAN + SEQ, None)
    in_specs = (tokens,) * 5 + (P(None, CHAN), P(CHAN), P(CHAN), rows, rows)
    return jax.shard_map(
        shards, mesh=fine, in_specs=in_specs, out_specs=(tokens,) * 4, check_vma=False
    )
```

```python
import jax
import jax.numpy as jnp
from jax import lax
from jax.experimental import pallas as pl
from jax.experimental.pallas import tpu as pltpu
from jax.sharding import Mesh, PartitionSpec as P

LEVELS = 16
SEQ = ("z", "y")
CHAN = ("x", "k")
SUB = 8
F32 = jnp.float32
BF16 = jnp.bfloat16
VMEM_LIMIT = 24 * 1024 * 1024
VMEM_WHOLE = 61 * 1024 * 1024


def decay_table(length):
    levels = jnp.arange(LEVELS).astype(F32)
    half = LEVELS // 2
    slow_rates = 0.25 * jnp.power(16.0, levels / (half - 1.0)) / (8.0 * length)
    fast_rates = jnp.power(4.0, (levels - half) / (half - 1.0)) / 640.0
    return -jnp.where(levels < half, slow_rates, fast_rates)


def gelu_parts(gate):
    normal_cdf = 0.5 * (1.0 + lax.erf(gate * 0.7071067811865476))
    density = jnp.exp(-0.5 * gate * gate) * 0.3989422804014327
    return (gate * normal_cdf, normal_cdf + gate * density)


def sigmoid(value):
    return 1.0 / (1.0 + jnp.exp(-value))


def expm1(value):
    series = jnp.ones_like(value)
    for term in range(9, 1, -1):
        series = 1.0 + value * (1.0 / term) * series
    return jnp.where(jnp.abs(value) < 0.5, value * series, jnp.exp(value) - 1.0)


def local_scan(a, b, reverse, a_out, b_out):
    rows, width = a.shape
    tiles = rows // SUB
    a = a.reshape(tiles, SUB, width)
    b = b.reshape(tiles, SUB, width)
    row = lax.broadcasted_iota(jnp.int32, a.shape, 1)
    for step in (1, 2, 4):
        shift = SUB - step if reverse else step
        inside = row < SUB - step if reverse else row >= step
        a_from = jnp.where(inside, pltpu.roll(a, shift, 1), 1.0)
        b_from = jnp.where(inside, pltpu.roll(b, shift, 1), 0.0)
        b = b + a * b_from
        a = a * a_from
    prod = jnp.ones((1, width), F32)
    state = jnp.zeros((1, width), F32)
    edge = 0 if reverse else SUB - 1
    for tile in reversed(range(tiles)) if reverse else range(tiles):
        here_b = b[tile] + a[tile] * state
        here_a = a[tile] * prod
        b_out[pl.ds(tile * SUB, SUB), :] = here_b
        a_out[pl.ds(tile * SUB, SUB), :] = here_a
        state = here_b[edge : edge + 1]
        prod = here_a[edge : edge + 1]
    return prod, state


def shift_up(value, last):
    rows = value.shape[0]
    row = lax.broadcasted_iota(jnp.int32, value.shape, 0)
    return jnp.where(row == rows - 1, last, pltpu.roll(value, rows - 1, 0))


def before_kernel(
    x_ref, prev_ref, rec_ref, inw_ref, cw_ref, cb_ref, ld_ref,
    decay_ref, beta_ref, conv_ref, cum_ref, local_ref, post_ref, slope_ref, ends_ref, front_ref,
    padded, scan_a, scan_b,
):
    rows = x_ref.shape[0]
    lead = prev_ref.shape[0]
    padded[pl.ds(0, lead), :] = prev_ref[...].astype(F32)
    padded[pl.ds(lead, rows), :] = x_ref[...].astype(F32)
    conv = jnp.zeros(x_ref.shape, F32)
    for lag in range(4):
        conv = conv + cw_ref[lag : lag + 1, :] * padded[pl.ds(lead - lag, rows), :]
    conv = cb_ref[...] + conv
    recur = sigmoid(rec_ref[...].astype(F32))
    inward = sigmoid(inw_ref[...].astype(F32))
    log_step = 8.0 * recur * ld_ref[...]
    decay = jnp.exp(log_step)
    beta = jnp.sqrt(-expm1(2.0 * log_step))
    decay_ref[...] = decay
    beta_ref[...] = beta
    conv_ref[...] = conv
    prod, state = local_scan(decay, beta * (inward * conv), False, cum_ref, local_ref)
    ends_ref[...] = jnp.concatenate([prod, state], axis=0)
    local_scan(decay, jnp.zeros_like(decay), True, scan_a, scan_b)
    post = shift_up(scan_a[...], 1.0)
    post_ref[...] = post
    slope = post * beta * inward
    slope_ref[...] = slope
    front_ref[...] = slope[:SUB]


def before(
    x_branch, prev, recurrence_gate, input_gate, conv_weight, conv_bias, log_decay
):
    rows, width = x_branch.shape
    full = jax.ShapeDtypeStruct((rows, width), F32)
    return pl.pallas_call(
        before_kernel,
        out_shape=(full,) * 7
        + (
            jax.ShapeDtypeStruct((2, width), F32),
            jax.ShapeDtypeStruct((SUB, width), F32),
        ),
        scratch_shapes=[
            pltpu.VMEM((rows + prev.shape[0], width), F32),
            pltpu.VMEM((rows, width), F32),
            pltpu.VMEM((rows, width), F32),
        ],
        compiler_params=pltpu.CompilerParams(vmem_limit_bytes=VMEM_LIMIT),
    )(x_branch, prev, recurrence_gate, input_gate, conv_weight, conv_bias, log_decay)


def partial_kernel(rows_ref, w_ref, out_ref):
    for i in range(rows_ref.shape[0]):
        out_ref[i] = lax.dot_general(
            rows_ref[i], w_ref[...], (((1,), (1,)), ((), ())), preferred_element_type=F32
        ).astype(BF16)


def partial_products(blocks, weights):
    count, rows, width = blocks.shape
    return pl.pallas_call(
        partial_kernel,
        grid=(count // 2,),
        in_specs=[
            pl.BlockSpec((2, rows, width), lambda i: (i, 0, 0)),
            pl.BlockSpec(weights.shape, lambda i: (0, 0)),
        ],
        out_specs=pl.BlockSpec((2, rows, weights.shape[0]), lambda i: (i, 0, 0)),
        out_shape=jax.ShapeDtypeStruct((count, rows, weights.shape[0]), BF16),
        compiler_params=pltpu.CompilerParams(vmem_limit_bytes=VMEM_WHOLE),
    )(blocks, weights)


def total_kernel(parts_ref, out_ref):
    total = parts_ref[0].astype(F32)
    for i in range(1, parts_ref.shape[0]):
        total = total + parts_ref[i].astype(F32)
    out_ref[...] = total.astype(BF16)


def total_of(parts):
    return pl.pallas_call(
        total_kernel,
        out_shape=jax.ShapeDtypeStruct(parts.shape[1:], BF16),
        compiler_params=pltpu.CompilerParams(vmem_limit_bytes=VMEM_LIMIT),
    )(parts)


def adjoint_kernel(
    dlru_ref, gate_ref, decay_ref, beta_ref, inw_ref, ends_ref,
    adj_ref, offset_ref, front_ref, carry_ref,
    scan_a, scan_b,
):
    d_direct = dlru_ref[...].astype(F32) * gelu_parts(gate_ref[...].astype(F32))[0]
    decay = decay_ref[...]
    _, first = local_scan(decay, decay * d_direct, True, scan_a, scan_b)
    adj = d_direct + shift_up(scan_b[...], 0.0)
    adj_ref[...] = adj
    offset = adj * beta_ref[...] * sigmoid(inw_ref[...].astype(F32))
    offset_ref[...] = offset
    front_ref[...] = offset[:SUB]
    mine = jnp.concatenate([ends_ref[...], first], axis=0)
    carry_ref[...] = jnp.broadcast_to(mine[None], carry_ref.shape)


def adjoint(d_lru, gate, decay, beta, input_gate, ends, seq_count):
    rows, width = gate.shape
    full = jax.ShapeDtypeStruct((rows, width), F32)
    return pl.pallas_call(
        adjoint_kernel,
        out_shape=(
            full,
            full,
            jax.ShapeDtypeStruct((SUB, width), F32),
            jax.ShapeDtypeStruct((seq_count, 3, width), F32),
        ),
        scratch_shapes=[pltpu.VMEM((rows, width), F32)] * 2,
        compiler_params=pltpu.CompilerParams(vmem_limit_bytes=VMEM_LIMIT),
    )(d_lru, gate, decay, beta, input_gate, ends)


def branch_kernel(
    place_ref, carry_ref, offset_ref, slope_ref, cw_ref, front_a_ref, front_b_ref,
    branch_ref, kappa_ref,
    padded,
):
    rows, width = offset_ref.shape
    place = place_ref[0]
    beyond = jnp.zeros((1, width), F32)
    kappa = jnp.zeros((1, width), F32)
    for i in reversed(range(1, carry_ref.shape[0])):
        here = carry_ref[i, 2:3] + carry_ref[i, 0:1] * kappa
        beyond = jnp.where(i == place + 1, kappa, beyond)
        kappa = jnp.where(i > place, here, kappa)
    padded[pl.ds(0, rows), :] = offset_ref[...] + slope_ref[...] * kappa
    padded[pl.ds(rows, SUB), :] = front_a_ref[...] + front_b_ref[...] * beyond
    total = jnp.zeros((rows, width), F32)
    for lag in range(4):
        total = total + cw_ref[lag : lag + 1, :] * padded[pl.ds(lag, rows), :]
    branch_ref[...] = total.astype(BF16)
    kappa_ref[...] = kappa


def branch(place, carry, offset, slope, conv_weight, front_a, front_b):
    rows, width = offset.shape
    vmem = pl.BlockSpec(memory_space=pltpu.VMEM)
    return pl.pallas_call(
        branch_kernel,
        in_specs=[pl.BlockSpec(memory_space=pltpu.SMEM)] + [vmem] * 6,
        out_shape=(
            jax.ShapeDtypeStruct((rows, width), BF16),
            jax.ShapeDtypeStruct((1, width), F32),
        ),
        scratch_shapes=[pltpu.VMEM((rows + SUB, width), F32)],
        compiler_params=pltpu.CompilerParams(vmem_limit_bytes=VMEM_LIMIT),
    )(place, carry, offset, slope, conv_weight, front_a, front_b)


def gates_kernel(
    place_ref, carry_ref, kappa_ref, dlru_ref, adj_ref, post_ref, cum_ref, local_ref, decay_ref,
    beta_ref, conv_ref, gate_ref, rec_ref, inw_ref, ld_ref,
    dgate_ref, drec_ref, dinw_ref,
):
    place = place_ref[0]
    carried = jnp.zeros(kappa_ref.shape, F32)
    for i in range(carry_ref.shape[0] - 1):
        carried = jnp.where(i < place, carry_ref[i, 1:2] + carry_ref[i, 0:1] * carried, carried)
    states = local_ref[...] + cum_ref[...] * carried
    slope = gelu_parts(gate_ref[...].astype(F32))[1]
    dgate_ref[...] = (dlru_ref[...].astype(F32) * states * slope).astype(BF16)
    row = lax.broadcasted_iota(jnp.int32, states.shape, 0)
    states_prev = jnp.where(row == 0, carried, pltpu.roll(states, 1, 0))
    recur = sigmoid(rec_ref[...].astype(F32))
    inward = sigmoid(inw_ref[...].astype(F32))
    decay = decay_ref[...]
    beta = beta_ref[...]
    conv = conv_ref[...]
    adj = adj_ref[...] + post_ref[...] * kappa_ref[...]
    d_step = adj * (decay * states_prev - inward * conv * decay * decay / beta)
    drec_ref[...] = (d_step * 8.0 * ld_ref[...] * recur * (1.0 - recur)).astype(BF16)
    dinw_ref[...] = (adj * beta * conv * inward * (1.0 - inward)).astype(BF16)


def gates(place, carry, kappa, d_lru, *arrays):
    out = jax.ShapeDtypeStruct(d_lru.shape, BF16)
    vmem = pl.BlockSpec(memory_space=pltpu.VMEM)
    return pl.pallas_call(
        gates_kernel,
        in_specs=[pl.BlockSpec(memory_space=pltpu.SMEM)] + [vmem] * (3 + len(arrays)),
        out_shape=(out,) * 3,
        compiler_params=pltpu.CompilerParams(vmem_limit_bytes=VMEM_LIMIT),
    )(place, carry, kappa, d_lru, *arrays)


def input_kernel(core_ref, own_ref, other_ref, w_ref, out_ref, acc):
    step = pl.program_id(0)
    half = w_ref.shape[1] // 2

    @pl.when(step == 0)
    def _():
        acc[...] = jnp.zeros_like(acc)

    def add(first, second):
        dims = (((1,), (1,)), ((), ()))
        acc[...] += lax.dot_general(
            first, w_ref[:, :half], dims, preferred_element_type=F32
        ) + lax.dot_general(second, w_ref[:, half:], dims, preferred_element_type=F32)

    @pl.when(core_ref[0] == 0)
    def _():
        add(own_ref[0], other_ref[0])

    @pl.when(core_ref[0] != 0)
    def _():
        add(other_ref[0], own_ref[0])

    @pl.when(step == pl.num_programs(0) - 1)
    def _():
        out_ref[...] = acc[...].astype(BF16)


def input_grad(core, own, other, weights):
    steps, rows, width = own.shape
    return pl.pallas_call(
        input_kernel,
        grid=(steps,),
        in_specs=[
            pl.BlockSpec(memory_space=pltpu.SMEM),
            pl.BlockSpec((1, rows, width), lambda i: (i, 0, 0)),
            pl.BlockSpec((1, rows, width), lambda i: (i, 0, 0)),
            pl.BlockSpec((weights.shape[0], 2 * width), lambda i: (0, i)),
        ],
        out_specs=pl.BlockSpec((rows, weights.shape[0]), lambda i: (0, 0)),
        out_shape=jax.ShapeDtypeStruct((rows, weights.shape[0]), BF16),
        scratch_shapes=[pltpu.VMEM((rows, weights.shape[0]), F32)],
        compiler_params=pltpu.CompilerParams(vmem_limit_bytes=VMEM_WHOLE),
    )(core, own, other, weights)


def shards(
    d_out,
    x_branch,
    gate_branch,
    recurrence_gate,
    input_gate,
    conv_weight,
    conv_bias,
    decay_level,
    w_in,
    w_out,
):
    tok_rows, width = x_branch.shape
    z_count, y_count = lax.axis_size("z"), lax.axis_size("y")
    seq_count, chan_count = lax.axis_size(SEQ), lax.axis_size(CHAN)
    w_rows = w_out.shape[0]
    place = lax.axis_index(SEQ).astype(jnp.int32).reshape(1)
    core = lax.axis_index("k").astype(jnp.int32).reshape(1)
    forward = [(i, i + 1) for i in range(seq_count - 1)]
    backward = [(i + 1, i) for i in range(seq_count - 1)]
    swap = [(y * chan_count + c, c * chan_count + y) for y in range(y_count) for c in range(chan_count)]

    blocks = lax.all_gather(d_out, "y")
    pieces = lax.all_to_all(w_out.reshape(w_rows, chan_count, width), CHAN, 1, 0)
    spread = jnp.broadcast_to(pieces[None], (z_count,) + pieces.shape)
    out_block = lax.all_to_all(spread.reshape(seq_count, w_rows, width), SEQ, 0, 0)
    prev = lax.ppermute(x_branch[tok_rows - 16 :], SEQ, forward)
    log_table = decay_table(tok_rows * seq_count)
    onehot = decay_level[:, None] == jnp.arange(LEVELS)[None, :]
    log_decay = jnp.sum(jnp.where(onehot, log_table[None, :], 0.0), axis=1)[None, :]
    decay, beta, conv_out, cum_decay, local_states, post, slope, ends, front_b = before(
        x_branch, prev, recurrence_gate, input_gate, conv_weight, conv_bias[None, :], log_decay
    )

    next_b = lax.ppermute(front_b, SEQ, backward)

    blocks, w_in, out_block, ends, next_b = lax.optimization_barrier(
        (blocks, w_in, out_block, ends, next_b)
    )
    in_rows = lax.all_gather(w_in, SEQ, axis=0, tiled=True)
    partial = partial_products(blocks, out_block.reshape(seq_count * w_rows, width))
    total = total_of(lax.all_to_all(partial, CHAN, 0, 0))
    d_lru = lax.ppermute(total, ("y",) + CHAN, swap)
    adj_local, offset, front_a, carry = adjoint(
        d_lru, gate_branch, decay, beta, input_gate, ends, seq_count
    )
    next_a = lax.ppermute(front_a, SEQ, backward)
    carries = lax.all_to_all(carry, SEQ, 0, 0)
    d_branch, kappa = branch(place, carries, offset, slope, conv_weight, next_a, next_b)
    own = lax.all_gather(d_branch, "x")
    other = lax.ppermute(own, "k", [(0, 1), (1, 0)])
    d_gate, d_recurrence_gate, d_input_gate = gates(
        place, carries, kappa, d_lru, adj_local, post, cum_decay, local_states, decay,
        beta, conv_out, gate_branch, recurrence_gate, input_gate, log_decay,
    )
    d_input = input_grad(core, own, other, in_rows)
    return (d_input, d_gate, d_recurrence_gate, d_input_gate)


def solution(mesh):
    fine = Mesh(mesh.devices.reshape(8, 8, 4, 2), SEQ + CHAN)
    tokens = P(SEQ, CHAN)
    rows = P(CHAN + SEQ, None)
    in_specs = (tokens,) * 5 + (P(None, CHAN), P(CHAN), P(CHAN), rows, rows)
    return jax.shard_map(
        shards, mesh=fine, in_specs=in_specs, out_specs=(tokens,) * 4, check_vma=False
    )
```

```python
import jax
import jax.numpy as jnp
from jax import lax
from jax.experimental import pallas as pl
from jax.experimental.pallas import tpu as pltpu
from jax.sharding import Mesh, PartitionSpec as P

LEVELS = 16
SEQ = ("z", "y")
CHAN = ("x", "k")
SUB = 8
F32 = jnp.float32
BF16 = jnp.bfloat16
VMEM_LIMIT = 24 * 1024 * 1024
VMEM_WHOLE = 61 * 1024 * 1024


def decay_table(length):
    levels = jnp.arange(LEVELS).astype(F32)
    half = LEVELS // 2
    slow_rates = 0.25 * jnp.power(16.0, levels / (half - 1.0)) / (8.0 * length)
    fast_rates = jnp.power(4.0, (levels - half) / (half - 1.0)) / 640.0
    return -jnp.where(levels < half, slow_rates, fast_rates)


def gelu_parts(gate):
    normal_cdf = 0.5 * (1.0 + lax.erf(gate * 0.7071067811865476))
    density = jnp.exp(-0.5 * gate * gate) * 0.3989422804014327
    return (gate * normal_cdf, normal_cdf + gate * density)


def sigmoid(value):
    return 1.0 / (1.0 + jnp.exp(-value))


def expm1(value):
    series = jnp.ones_like(value)
    for term in range(9, 1, -1):
        series = 1.0 + value * (1.0 / term) * series
    return jnp.where(jnp.abs(value) < 0.5, value * series, jnp.exp(value) - 1.0)


def local_scan(a, b, reverse, a_out, b_out):
    rows, width = a.shape
    tiles = rows // SUB
    a = a.reshape(tiles, SUB, width)
    b = b.reshape(tiles, SUB, width)
    row = lax.broadcasted_iota(jnp.int32, a.shape, 1)
    for step in (1, 2, 4):
        shift = SUB - step if reverse else step
        inside = row < SUB - step if reverse else row >= step
        a_from = jnp.where(inside, pltpu.roll(a, shift, 1), 1.0)
        b_from = jnp.where(inside, pltpu.roll(b, shift, 1), 0.0)
        b = b + a * b_from
        a = a * a_from
    prod = jnp.ones((1, width), F32)
    state = jnp.zeros((1, width), F32)
    edge = 0 if reverse else SUB - 1
    for tile in reversed(range(tiles)) if reverse else range(tiles):
        here_b = b[tile] + a[tile] * state
        here_a = a[tile] * prod
        b_out[pl.ds(tile * SUB, SUB), :] = here_b
        a_out[pl.ds(tile * SUB, SUB), :] = here_a
        state = here_b[edge : edge + 1]
        prod = here_a[edge : edge + 1]
    return prod, state


def shift_up(value, last):
    rows = value.shape[0]
    row = lax.broadcasted_iota(jnp.int32, value.shape, 0)
    return jnp.where(row == rows - 1, last, pltpu.roll(value, rows - 1, 0))


def before_kernel(
    x_ref, prev_ref, rec_ref, inw_ref, cw_ref, cb_ref, ld_ref,
    decay_ref, beta_ref, conv_ref, cum_ref, local_ref, post_ref, slope_ref, ends_ref, front_ref,
    padded, scan_a, scan_b,
):
    rows = x_ref.shape[0]
    lead = prev_ref.shape[0]
    padded[pl.ds(0, lead), :] = prev_ref[...].astype(F32)
    padded[pl.ds(lead, rows), :] = x_ref[...].astype(F32)
    conv = jnp.zeros(x_ref.shape, F32)
    for lag in range(4):
        conv = conv + cw_ref[lag : lag + 1, :] * padded[pl.ds(lead - lag, rows), :]
    conv = cb_ref[...] + conv
    recur = sigmoid(rec_ref[...].astype(F32))
    inward = sigmoid(inw_ref[...].astype(F32))
    log_step = 8.0 * recur * ld_ref[...]
    decay = jnp.exp(log_step)
    beta = jnp.sqrt(-expm1(2.0 * log_step))
    decay_ref[...] = decay
    beta_ref[...] = beta
    conv_ref[...] = conv
    prod, state = local_scan(decay, beta * (inward * conv), False, cum_ref, local_ref)
    ends_ref[...] = jnp.concatenate([prod, state], axis=0)
    local_scan(decay, jnp.zeros_like(decay), True, scan_a, scan_b)
    post = shift_up(scan_a[...], 1.0)
    post_ref[...] = post
    slope = post * beta * inward
    slope_ref[...] = slope
    front_ref[...] = slope[:SUB]


def before(
    x_branch, prev, recurrence_gate, input_gate, conv_weight, conv_bias, log_decay
):
    rows, width = x_branch.shape
    full = jax.ShapeDtypeStruct((rows, width), F32)
    return pl.pallas_call(
        before_kernel,
        out_shape=(full,) * 7
        + (
            jax.ShapeDtypeStruct((2, width), F32),
            jax.ShapeDtypeStruct((SUB, width), F32),
        ),
        scratch_shapes=[
            pltpu.VMEM((rows + prev.shape[0], width), F32),
            pltpu.VMEM((rows, width), F32),
            pltpu.VMEM((rows, width), F32),
        ],
        compiler_params=pltpu.CompilerParams(vmem_limit_bytes=VMEM_LIMIT),
    )(x_branch, prev, recurrence_gate, input_gate, conv_weight, conv_bias, log_decay)


def adjoint_kernel(
    core_ref, own_ref, other_ref, w_ref, gate_ref, decay_ref, beta_ref, inw_ref, ends_ref,
    dlru_ref, adj_ref, offset_ref, front_ref, carry_ref,
    acc, scan_a, scan_b,
):
    step = pl.program_id(0)
    half = w_ref.shape[1] // 2

    @pl.when(step == 0)
    def _():
        acc[...] = jnp.zeros_like(acc)

    def add(first, second):
        dims = (((1,), (1,)), ((), ()))
        acc[...] += lax.dot_general(
            first, w_ref[:, :half], dims, preferred_element_type=F32
        ) + lax.dot_general(second, w_ref[:, half:], dims, preferred_element_type=F32)

    @pl.when(core_ref[0] == 0)
    def _():
        add(own_ref[0], other_ref[0])

    @pl.when(core_ref[0] != 0)
    def _():
        add(other_ref[0], own_ref[0])

    @pl.when(step == pl.num_programs(0) - 1)
    def _():
        d_lru = acc[...]
        dlru_ref[...] = d_lru
        d_direct = d_lru * gelu_parts(gate_ref[...].astype(F32))[0]
        decay = decay_ref[...]
        _, first = local_scan(decay, decay * d_direct, True, scan_a, scan_b)
        adj = d_direct + shift_up(scan_b[...], 0.0)
        adj_ref[...] = adj
        offset = adj * beta_ref[...] * sigmoid(inw_ref[...].astype(F32))
        offset_ref[...] = offset
        front_ref[...] = offset[:SUB]
        mine = jnp.concatenate([ends_ref[...], first], axis=0)
        carry_ref[...] = jnp.broadcast_to(mine[None], carry_ref.shape)


def adjoint(core, own, other, weights, gate, decay, beta, input_gate, ends, seq_count):
    rows, width = gate.shape
    steps = own.shape[0]
    full = jax.ShapeDtypeStruct((rows, width), F32)
    whole = lambda shape: pl.BlockSpec(shape, lambda i: (0,) * len(shape))
    return pl.pallas_call(
        adjoint_kernel,
        grid=(steps,),
        in_specs=[
            pl.BlockSpec(memory_space=pltpu.SMEM),
            pl.BlockSpec((1, rows, width), lambda i: (i, 0, 0)),
            pl.BlockSpec((1, rows, width), lambda i: (i, 0, 0)),
            pl.BlockSpec((width, 2 * width), lambda i: (0, i)),
            whole((rows, width)),
            whole((rows, width)),
            whole((rows, width)),
            whole((rows, width)),
            whole((2, width)),
        ],
        out_specs=[
            whole((rows, width)),
            whole((rows, width)),
            whole((rows, width)),
            whole((SUB, width)),
            whole((seq_count, 3, width)),
        ],
        out_shape=(
            full,
            full,
            full,
            jax.ShapeDtypeStruct((SUB, width), F32),
            jax.ShapeDtypeStruct((seq_count, 3, width), F32),
        ),
        scratch_shapes=[pltpu.VMEM((rows, width), F32)] * 3,
        compiler_params=pltpu.CompilerParams(vmem_limit_bytes=VMEM_WHOLE),
    )(core, own, other, weights, gate, decay, beta, input_gate, ends)


def branch_kernel(
    place_ref, carry_ref, offset_ref, slope_ref, cw_ref, front_a_ref, front_b_ref,
    branch_ref, kappa_ref,
    padded,
):
    rows, width = offset_ref.shape
    place = place_ref[0]
    beyond = jnp.zeros((1, width), F32)
    kappa = jnp.zeros((1, width), F32)
    for i in reversed(range(1, carry_ref.shape[0])):
        here = carry_ref[i, 2:3] + carry_ref[i, 0:1] * kappa
        beyond = jnp.where(i == place + 1, kappa, beyond)
        kappa = jnp.where(i > place, here, kappa)
    padded[pl.ds(0, rows), :] = offset_ref[...] + slope_ref[...] * kappa
    padded[pl.ds(rows, SUB), :] = front_a_ref[...] + front_b_ref[...] * beyond
    total = jnp.zeros((rows, width), F32)
    for lag in range(4):
        total = total + cw_ref[lag : lag + 1, :] * padded[pl.ds(lag, rows), :]
    branch_ref[...] = total.astype(BF16)
    kappa_ref[...] = kappa


def branch(place, carry, offset, slope, conv_weight, front_a, front_b):
    rows, width = offset.shape
    vmem = pl.BlockSpec(memory_space=pltpu.VMEM)
    return pl.pallas_call(
        branch_kernel,
        in_specs=[pl.BlockSpec(memory_space=pltpu.SMEM)] + [vmem] * 6,
        out_shape=(
            jax.ShapeDtypeStruct((rows, width), BF16),
            jax.ShapeDtypeStruct((1, width), F32),
        ),
        scratch_shapes=[pltpu.VMEM((rows + SUB, width), F32)],
        compiler_params=pltpu.CompilerParams(vmem_limit_bytes=VMEM_LIMIT),
    )(place, carry, offset, slope, conv_weight, front_a, front_b)


def gates_kernel(
    place_ref, carry_ref, kappa_ref, dlru_ref, adj_ref, post_ref, cum_ref, local_ref, decay_ref,
    beta_ref, conv_ref, gate_ref, rec_ref, inw_ref, ld_ref,
    dgate_ref, drec_ref, dinw_ref,
):
    place = place_ref[0]
    carried = jnp.zeros(kappa_ref.shape, F32)
    for i in range(carry_ref.shape[0] - 1):
        carried = jnp.where(i < place, carry_ref[i, 1:2] + carry_ref[i, 0:1] * carried, carried)
    states = local_ref[...] + cum_ref[...] * carried
    slope = gelu_parts(gate_ref[...].astype(F32))[1]
    dgate_ref[...] = (dlru_ref[...].astype(F32) * states * slope).astype(BF16)
    row = lax.broadcasted_iota(jnp.int32, states.shape, 0)
    states_prev = jnp.where(row == 0, carried, pltpu.roll(states, 1, 0))
    recur = sigmoid(rec_ref[...].astype(F32))
    inward = sigmoid(inw_ref[...].astype(F32))
    decay = decay_ref[...]
    beta = beta_ref[...]
    conv = conv_ref[...]
    adj = adj_ref[...] + post_ref[...] * kappa_ref[...]
    d_step = adj * (decay * states_prev - inward * conv * decay * decay / beta)
    drec_ref[...] = (d_step * 8.0 * ld_ref[...] * recur * (1.0 - recur)).astype(BF16)
    dinw_ref[...] = (adj * beta * conv * inward * (1.0 - inward)).astype(BF16)


def gates(place, carry, kappa, d_lru, *arrays):
    out = jax.ShapeDtypeStruct(d_lru.shape, BF16)
    vmem = pl.BlockSpec(memory_space=pltpu.VMEM)
    return pl.pallas_call(
        gates_kernel,
        in_specs=[pl.BlockSpec(memory_space=pltpu.SMEM)] + [vmem] * (3 + len(arrays)),
        out_shape=(out,) * 3,
        compiler_params=pltpu.CompilerParams(vmem_limit_bytes=VMEM_LIMIT),
    )(place, carry, kappa, d_lru, *arrays)


def input_kernel(core_ref, own_ref, other_ref, w_ref, out_ref, acc):
    step = pl.program_id(0)
    half = w_ref.shape[1] // 2

    @pl.when(step == 0)
    def _():
        acc[...] = jnp.zeros_like(acc)

    def add(first, second):
        dims = (((1,), (1,)), ((), ()))
        acc[...] += lax.dot_general(
            first, w_ref[:, :half], dims, preferred_element_type=F32
        ) + lax.dot_general(second, w_ref[:, half:], dims, preferred_element_type=F32)

    @pl.when(core_ref[0] == 0)
    def _():
        add(own_ref[0], other_ref[0])

    @pl.when(core_ref[0] != 0)
    def _():
        add(other_ref[0], own_ref[0])

    @pl.when(step == pl.num_programs(0) - 1)
    def _():
        out_ref[...] = acc[...].astype(BF16)


def input_grad(core, own, other, weights):
    steps, rows, width = own.shape
    return pl.pallas_call(
        input_kernel,
        grid=(steps,),
        in_specs=[
            pl.BlockSpec(memory_space=pltpu.SMEM),
            pl.BlockSpec((1, rows, width), lambda i: (i, 0, 0)),
            pl.BlockSpec((1, rows, width), lambda i: (i, 0, 0)),
            pl.BlockSpec((weights.shape[0], 2 * width), lambda i: (0, i)),
        ],
        out_specs=pl.BlockSpec((rows, weights.shape[0]), lambda i: (0, 0)),
        out_shape=jax.ShapeDtypeStruct((rows, weights.shape[0]), BF16),
        scratch_shapes=[pltpu.VMEM((rows, weights.shape[0]), F32)],
        compiler_params=pltpu.CompilerParams(vmem_limit_bytes=VMEM_WHOLE),
    )(core, own, other, weights)


def shards(
    d_out,
    x_branch,
    gate_branch,
    recurrence_gate,
    input_gate,
    conv_weight,
    conv_bias,
    decay_level,
    w_in,
    w_out,
):
    tok_rows, width = x_branch.shape
    seq_count = lax.axis_size(SEQ)
    place = lax.axis_index(SEQ).astype(jnp.int32).reshape(1)
    core = lax.axis_index("k").astype(jnp.int32).reshape(1)
    forward = [(i, i + 1) for i in range(seq_count - 1)]
    backward = [(i + 1, i) for i in range(seq_count - 1)]
    cores = [(0, 1), (1, 0)]

    out_rows = lax.all_gather(w_out, SEQ, axis=0, tiled=True)
    in_part = lax.all_gather(w_in, "y", axis=0, tiled=True)
    in_rows = lax.all_gather(in_part, "z", axis=0, tiled=True)
    out_own = lax.all_gather(d_out, "x")
    out_other = lax.ppermute(out_own, "k", cores)
    prev = lax.ppermute(x_branch[tok_rows - 16 :], SEQ, forward)
    log_table = decay_table(tok_rows * seq_count)
    onehot = decay_level[:, None] == jnp.arange(LEVELS)[None, :]
    log_decay = jnp.sum(jnp.where(onehot, log_table[None, :], 0.0), axis=1)[None, :]
    decay, beta, conv_out, cum_decay, local_states, post, slope, ends, front_b = before(
        x_branch, prev, recurrence_gate, input_gate, conv_weight, conv_bias[None, :], log_decay
    )

    next_b = lax.ppermute(front_b, SEQ, backward)

    ends, next_b, in_part = lax.optimization_barrier((ends, next_b, in_part))
    d_lru, adj_local, offset, front_a, carry = adjoint(
        core, out_own, out_other, out_rows, gate_branch, decay, beta, input_gate, ends, seq_count
    )
    next_a = lax.ppermute(front_a, SEQ, backward)
    carries = lax.all_to_all(carry, SEQ, 0, 0)
    d_branch, kappa = branch(place, carries, offset, slope, conv_weight, next_a, next_b)
    own = lax.all_gather(d_branch, "x")
    other = lax.ppermute(own, "k", cores)
    d_gate, d_recurrence_gate, d_input_gate = gates(
        place, carries, kappa, d_lru, adj_local, post, cum_decay, local_states, decay,
        beta, conv_out, gate_branch, recurrence_gate, input_gate, log_decay,
    )
    d_input = input_grad(core, own, other, in_rows)
    return (d_input, d_gate, d_recurrence_gate, d_input_gate)


def solution(mesh):
    fine = Mesh(mesh.devices.reshape(8, 8, 4, 2), SEQ + CHAN)
    tokens = P(SEQ, CHAN)
    rows = P(CHAN + SEQ, None)
    in_specs = (tokens,) * 5 + (P(None, CHAN), P(CHAN), P(CHAN), rows, rows)
    return jax.shard_map(
        shards, mesh=fine, in_specs=in_specs, out_specs=(tokens,) * 4, check_vma=False
    )
```

```python
import jax
import jax.numpy as jnp
from jax import lax
from jax.experimental import pallas as pl
from jax.experimental.pallas import tpu as pltpu
from jax.sharding import Mesh, PartitionSpec as P

LEVELS = 16
SEQ = ("z", "y")
CHAN = ("x", "k")
SUB = 8
F32 = jnp.float32
BF16 = jnp.bfloat16
VMEM_LIMIT = 24 * 1024 * 1024
VMEM_WHOLE = 61 * 1024 * 1024


def decay_table(length):
    levels = jnp.arange(LEVELS).astype(F32)
    half = LEVELS // 2
    slow_rates = 0.25 * jnp.power(16.0, levels / (half - 1.0)) / (8.0 * length)
    fast_rates = jnp.power(4.0, (levels - half) / (half - 1.0)) / 640.0
    return -jnp.where(levels < half, slow_rates, fast_rates)


def gelu_parts(gate):
    normal_cdf = 0.5 * (1.0 + lax.erf(gate * 0.7071067811865476))
    density = jnp.exp(-0.5 * gate * gate) * 0.3989422804014327
    return (gate * normal_cdf, normal_cdf + gate * density)


def sigmoid(value):
    return 1.0 / (1.0 + jnp.exp(-value))


def expm1(value):
    series = jnp.ones_like(value)
    for term in range(9, 1, -1):
        series = 1.0 + value * (1.0 / term) * series
    return jnp.where(jnp.abs(value) < 0.5, value * series, jnp.exp(value) - 1.0)


def local_scan(a, b, reverse, a_out, b_out):
    rows, width = a.shape
    tiles = rows // SUB
    a = a.reshape(tiles, SUB, width)
    b = b.reshape(tiles, SUB, width)
    row = lax.broadcasted_iota(jnp.int32, a.shape, 1)
    for step in (1, 2, 4):
        shift = SUB - step if reverse else step
        inside = row < SUB - step if reverse else row >= step
        a_from = jnp.where(inside, pltpu.roll(a, shift, 1), 1.0)
        b_from = jnp.where(inside, pltpu.roll(b, shift, 1), 0.0)
        b = b + a * b_from
        a = a * a_from
    prod = jnp.ones((1, width), F32)
    state = jnp.zeros((1, width), F32)
    edge = 0 if reverse else SUB - 1
    for tile in reversed(range(tiles)) if reverse else range(tiles):
        here_b = b[tile] + a[tile] * state
        here_a = a[tile] * prod
        b_out[pl.ds(tile * SUB, SUB), :] = here_b
        a_out[pl.ds(tile * SUB, SUB), :] = here_a
        state = here_b[edge : edge + 1]
        prod = here_a[edge : edge + 1]
    return prod, state


def shift_up(value, last):
    rows = value.shape[0]
    row = lax.broadcasted_iota(jnp.int32, value.shape, 0)
    return jnp.where(row == rows - 1, last, pltpu.roll(value, rows - 1, 0))


def before_kernel(
    x_ref, prev_ref, rec_ref, inw_ref, cw_ref, cb_ref, ld_ref,
    decay_ref, beta_ref, conv_ref, cum_ref, local_ref, post_ref, slope_ref, ends_ref, front_ref,
    padded, scan_a, scan_b,
):
    rows = x_ref.shape[0]
    lead = prev_ref.shape[0]
    padded[pl.ds(0, lead), :] = prev_ref[...].astype(F32)
    padded[pl.ds(lead, rows), :] = x_ref[...].astype(F32)
    conv = jnp.zeros(x_ref.shape, F32)
    for lag in range(4):
        conv = conv + cw_ref[lag : lag + 1, :] * padded[pl.ds(lead - lag, rows), :]
    conv = cb_ref[...] + conv
    recur = sigmoid(rec_ref[...].astype(F32))
    inward = sigmoid(inw_ref[...].astype(F32))
    log_step = 8.0 * recur * ld_ref[...]
    decay = jnp.exp(log_step)
    beta = jnp.sqrt(-expm1(2.0 * log_step))
    decay_ref[...] = decay
    beta_ref[...] = beta
    conv_ref[...] = conv
    prod, state = local_scan(decay, beta * (inward * conv), False, cum_ref, local_ref)
    ends_ref[...] = jnp.concatenate([prod, state], axis=0)
    local_scan(decay, jnp.zeros_like(decay), True, scan_a, scan_b)
    post = shift_up(scan_a[...], 1.0)
    post_ref[...] = post
    slope = post * beta * inward
    slope_ref[...] = slope
    front_ref[...] = slope[:SUB]


def before(
    x_branch, prev, recurrence_gate, input_gate, conv_weight, conv_bias, log_decay
):
    rows, width = x_branch.shape
    full = jax.ShapeDtypeStruct((rows, width), F32)
    return pl.pallas_call(
        before_kernel,
        out_shape=(full,) * 7
        + (
            jax.ShapeDtypeStruct((2, width), F32),
            jax.ShapeDtypeStruct((SUB, width), F32),
        ),
        scratch_shapes=[
            pltpu.VMEM((rows + prev.shape[0], width), F32),
            pltpu.VMEM((rows, width), F32),
            pltpu.VMEM((rows, width), F32),
        ],
        compiler_params=pltpu.CompilerParams(vmem_limit_bytes=VMEM_LIMIT),
    )(x_branch, prev, recurrence_gate, input_gate, conv_weight, conv_bias, log_decay)


def adjoint_kernel(
    core_ref, own_ref, other_ref, w_ref, gate_ref, decay_ref, beta_ref, inw_ref, ends_ref,
    dlru_ref, adj_ref, offset_ref, front_ref, carry_ref,
    acc, scan_a, scan_b,
):
    step = pl.program_id(0)
    half = w_ref.shape[1] // 2

    @pl.when(step == 0)
    def _():
        acc[...] = jnp.zeros_like(acc)

    def add(first, second):
        dims = (((1,), (1,)), ((), ()))
        acc[...] += lax.dot_general(
            first, w_ref[:, :half], dims, preferred_element_type=F32
        ) + lax.dot_general(second, w_ref[:, half:], dims, preferred_element_type=F32)

    @pl.when(core_ref[0] == 0)
    def _():
        add(own_ref[0], other_ref[0])

    @pl.when(core_ref[0] != 0)
    def _():
        add(other_ref[0], own_ref[0])

    @pl.when(step == pl.num_programs(0) - 1)
    def _():
        d_lru = acc[...]
        dlru_ref[...] = d_lru
        d_direct = d_lru * gelu_parts(gate_ref[...].astype(F32))[0]
        decay = decay_ref[...]
        _, first = local_scan(decay, decay * d_direct, True, scan_a, scan_b)
        adj = d_direct + shift_up(scan_b[...], 0.0)
        adj_ref[...] = adj
        offset = adj * beta_ref[...] * sigmoid(inw_ref[...].astype(F32))
        offset_ref[...] = offset
        front_ref[...] = offset[:SUB]
        mine = jnp.concatenate([ends_ref[...], first], axis=0)
        carry_ref[...] = jnp.broadcast_to(mine[None], carry_ref.shape)


def adjoint(core, own, other, weights, gate, decay, beta, input_gate, ends, seq_count):
    rows, width = gate.shape
    steps = own.shape[0]
    full = jax.ShapeDtypeStruct((rows, width), F32)
    whole = lambda shape: pl.BlockSpec(shape, lambda i: (0,) * len(shape))
    return pl.pallas_call(
        adjoint_kernel,
        grid=(steps,),
        in_specs=[
            pl.BlockSpec(memory_space=pltpu.SMEM),
            pl.BlockSpec((1, rows, width), lambda i: (i, 0, 0)),
            pl.BlockSpec((1, rows, width), lambda i: (i, 0, 0)),
            pl.BlockSpec((width, 2 * width), lambda i: (0, i)),
            whole((rows, width)),
            whole((rows, width)),
            whole((rows, width)),
            whole((rows, width)),
            whole((2, width)),
        ],
        out_specs=[
            whole((rows, width)),
            whole((rows, width)),
            whole((rows, width)),
            whole((SUB, width)),
            whole((seq_count, 3, width)),
        ],
        out_shape=(
            full,
            full,
            full,
            jax.ShapeDtypeStruct((SUB, width), F32),
            jax.ShapeDtypeStruct((seq_count, 3, width), F32),
        ),
        scratch_shapes=[pltpu.VMEM((rows, width), F32)] * 3,
        compiler_params=pltpu.CompilerParams(vmem_limit_bytes=VMEM_WHOLE),
    )(core, own, other, weights, gate, decay, beta, input_gate, ends)


def branch_kernel(
    place_ref, carry_ref, offset_ref, slope_ref, cw_ref, front_a_ref, front_b_ref,
    branch_ref, kappa_ref,
    padded,
):
    rows, width = offset_ref.shape
    place = place_ref[0]
    beyond = jnp.zeros((1, width), F32)
    kappa = jnp.zeros((1, width), F32)
    for i in reversed(range(1, carry_ref.shape[0])):
        here = carry_ref[i, 2:3] + carry_ref[i, 0:1] * kappa
        beyond = jnp.where(i == place + 1, kappa, beyond)
        kappa = jnp.where(i > place, here, kappa)
    padded[pl.ds(0, rows), :] = offset_ref[...] + slope_ref[...] * kappa
    padded[pl.ds(rows, SUB), :] = front_a_ref[...] + front_b_ref[...] * beyond
    total = jnp.zeros((rows, width), F32)
    for lag in range(4):
        total = total + cw_ref[lag : lag + 1, :] * padded[pl.ds(lag, rows), :]
    branch_ref[...] = total.astype(BF16)
    kappa_ref[...] = kappa


def branch(place, carry, offset, slope, conv_weight, front_a, front_b):
    rows, width = offset.shape
    vmem = pl.BlockSpec(memory_space=pltpu.VMEM)
    return pl.pallas_call(
        branch_kernel,
        in_specs=[pl.BlockSpec(memory_space=pltpu.SMEM)] + [vmem] * 6,
        out_shape=(
            jax.ShapeDtypeStruct((rows, width), BF16),
            jax.ShapeDtypeStruct((1, width), F32),
        ),
        scratch_shapes=[pltpu.VMEM((rows + SUB, width), F32)],
        compiler_params=pltpu.CompilerParams(vmem_limit_bytes=VMEM_LIMIT),
    )(place, carry, offset, slope, conv_weight, front_a, front_b)


def gates_kernel(
    place_ref, carry_ref, kappa_ref, dlru_ref, adj_ref, post_ref, cum_ref, local_ref, decay_ref,
    beta_ref, conv_ref, gate_ref, rec_ref, inw_ref, ld_ref,
    dgate_ref, drec_ref, dinw_ref,
):
    place = place_ref[0]
    carried = jnp.zeros(kappa_ref.shape, F32)
    for i in range(carry_ref.shape[0] - 1):
        carried = jnp.where(i < place, carry_ref[i, 1:2] + carry_ref[i, 0:1] * carried, carried)
    states = local_ref[...] + cum_ref[...] * carried
    slope = gelu_parts(gate_ref[...].astype(F32))[1]
    dgate_ref[...] = (dlru_ref[...].astype(F32) * states * slope).astype(BF16)
    row = lax.broadcasted_iota(jnp.int32, states.shape, 0)
    states_prev = jnp.where(row == 0, carried, pltpu.roll(states, 1, 0))
    recur = sigmoid(rec_ref[...].astype(F32))
    inward = sigmoid(inw_ref[...].astype(F32))
    decay = decay_ref[...]
    beta = beta_ref[...]
    conv = conv_ref[...]
    adj = adj_ref[...] + post_ref[...] * kappa_ref[...]
    d_step = adj * (decay * states_prev - inward * conv * decay * decay / beta)
    drec_ref[...] = (d_step * 8.0 * ld_ref[...] * recur * (1.0 - recur)).astype(BF16)
    dinw_ref[...] = (adj * beta * conv * inward * (1.0 - inward)).astype(BF16)


def gates(place, carry, kappa, d_lru, *arrays):
    out = jax.ShapeDtypeStruct(d_lru.shape, BF16)
    vmem = pl.BlockSpec(memory_space=pltpu.VMEM)
    return pl.pallas_call(
        gates_kernel,
        in_specs=[pl.BlockSpec(memory_space=pltpu.SMEM)] + [vmem] * (3 + len(arrays)),
        out_shape=(out,) * 3,
        compiler_params=pltpu.CompilerParams(vmem_limit_bytes=VMEM_LIMIT),
    )(place, carry, kappa, d_lru, *arrays)


def input_kernel(core_ref, own_ref, other_ref, first_ref, rest_ref, out_ref, acc):
    step = pl.program_id(0)
    half = first_ref.shape[1] // 2

    def product(left, right, w_ref):
        dims = (((1,), (1,)), ((), ()))
        return lax.dot_general(
            left, w_ref[:, :half], dims, preferred_element_type=F32
        ) + lax.dot_general(right, w_ref[:, half:], dims, preferred_element_type=F32)

    def add(left, right):
        @pl.when(step == 0)
        def _():
            acc[...] = product(left[0], right[0], first_ref)

        @pl.when(step != 0)
        def _():
            acc[...] += product(left[0], right[0], rest_ref)

    @pl.when(core_ref[0] == 0)
    def _():
        add(own_ref, other_ref)

    @pl.when(core_ref[0] != 0)
    def _():
        add(other_ref, own_ref)

    @pl.when(step == pl.num_programs(0) - 1)
    def _():
        out_ref[...] = acc[...].astype(BF16)


def input_grad(core, own, other, first, rest):
    steps, rows, width = own.shape
    feats = first.shape[0]
    at = first.shape[1] // (2 * width) - 1
    return pl.pallas_call(
        input_kernel,
        grid=(steps,),
        in_specs=[
            pl.BlockSpec(memory_space=pltpu.SMEM),
            pl.BlockSpec((1, rows, width), lambda i: (i, 0, 0)),
            pl.BlockSpec((1, rows, width), lambda i: (i, 0, 0)),
            pl.BlockSpec((feats, 2 * width), lambda i: (0, at)),
            pl.BlockSpec((feats, 2 * width), lambda i: (0, jnp.maximum(i - 1, 0))),
        ],
        out_specs=pl.BlockSpec((rows, feats), lambda i: (0, 0)),
        out_shape=jax.ShapeDtypeStruct((rows, feats), BF16),
        scratch_shapes=[pltpu.VMEM((rows, feats), F32)],
        compiler_params=pltpu.CompilerParams(vmem_limit_bytes=VMEM_WHOLE),
    )(core, own, other, first, rest)


def shards(
    d_out,
    x_branch,
    gate_branch,
    recurrence_gate,
    input_gate,
    conv_weight,
    conv_bias,
    decay_level,
    w_in,
    w_out,
):
    tok_rows, width = x_branch.shape
    seq_count = lax.axis_size(SEQ)
    place = lax.axis_index(SEQ).astype(jnp.int32).reshape(1)
    core = lax.axis_index("k").astype(jnp.int32).reshape(1)
    forward = [(i, i + 1) for i in range(seq_count - 1)]
    backward = [(i + 1, i) for i in range(seq_count - 1)]
    cores = [(0, 1), (1, 0)]

    first = jnp.concatenate([w_out, w_in[:, : 2 * width]], axis=1)
    first = lax.all_gather(first, SEQ, axis=0, tiled=True)
    rest = lax.all_gather(w_in[:, 2 * width :], "y", axis=0, tiled=True)
    in_rows = lax.all_gather(rest, "z", axis=0, tiled=True)
    out_own = lax.all_gather(d_out, "x")
    out_other = lax.ppermute(out_own, "k", cores)
    prev = lax.ppermute(x_branch[tok_rows - 16 :], SEQ, forward)
    log_table = decay_table(tok_rows * seq_count)
    onehot = decay_level[:, None] == jnp.arange(LEVELS)[None, :]
    log_decay = jnp.sum(jnp.where(onehot, log_table[None, :], 0.0), axis=1)[None, :]
    decay, beta, conv_out, cum_decay, local_states, post, slope, ends, front_b = before(
        x_branch, prev, recurrence_gate, input_gate, conv_weight, conv_bias[None, :], log_decay
    )

    next_b = lax.ppermute(front_b, SEQ, backward)

    ends, next_b = lax.optimization_barrier((ends, next_b))
    d_lru, adj_local, offset, front_a, carry = adjoint(
        core, out_own, out_other, first, gate_branch, decay, beta, input_gate, ends, seq_count
    )
    next_a = lax.ppermute(front_a, SEQ, backward)
    carries = lax.all_to_all(carry, SEQ, 0, 0)
    d_branch, kappa = branch(place, carries, offset, slope, conv_weight, next_a, next_b)
    own = lax.all_gather(d_branch, "x")
    other = lax.ppermute(own, "k", cores)
    d_gate, d_recurrence_gate, d_input_gate = gates(
        place, carries, kappa, d_lru, adj_local, post, cum_decay, local_states, decay,
        beta, conv_out, gate_branch, recurrence_gate, input_gate, log_decay,
    )
    d_input = input_grad(core, own, other, first, in_rows)
    return (d_input, d_gate, d_recurrence_gate, d_input_gate)


def solution(mesh):
    fine = Mesh(mesh.devices.reshape(8, 8, 4, 2), SEQ + CHAN)
    tokens = P(SEQ, CHAN)
    rows = P(CHAN + SEQ, None)
    in_specs = (tokens,) * 5 + (P(None, CHAN), P(CHAN), P(CHAN), rows, rows)
    return jax.shard_map(
        shards, mesh=fine, in_specs=in_specs, out_specs=(tokens,) * 4, check_vma=False
    )
```

```python
import jax
import jax.numpy as jnp
from jax import lax
from jax.experimental import pallas as pl
from jax.experimental.pallas import tpu as pltpu
from jax.sharding import Mesh, PartitionSpec as P

LEVELS = 16
SEQ = ("z", "y")
CHAN = ("x", "k")
SUB = 8
F32 = jnp.float32
BF16 = jnp.bfloat16
VMEM_LIMIT = 24 * 1024 * 1024
VMEM_WHOLE = 61 * 1024 * 1024


def decay_table(length):
    levels = jnp.arange(LEVELS).astype(F32)
    half = LEVELS // 2
    slow_rates = 0.25 * jnp.power(16.0, levels / (half - 1.0)) / (8.0 * length)
    fast_rates = jnp.power(4.0, (levels - half) / (half - 1.0)) / 640.0
    return -jnp.where(levels < half, slow_rates, fast_rates)


def gelu_parts(gate):
    normal_cdf = 0.5 * (1.0 + lax.erf(gate * 0.7071067811865476))
    density = jnp.exp(-0.5 * gate * gate) * 0.3989422804014327
    return (gate * normal_cdf, normal_cdf + gate * density)


def sigmoid(value):
    return 1.0 / (1.0 + jnp.exp(-value))


def expm1(value):
    series = jnp.ones_like(value)
    for term in range(9, 1, -1):
        series = 1.0 + value * (1.0 / term) * series
    return jnp.where(jnp.abs(value) < 0.5, value * series, jnp.exp(value) - 1.0)


def local_scan(a, b, reverse, a_out, b_out):
    rows, width = a.shape
    tiles = rows // SUB
    a = a.reshape(tiles, SUB, width)
    b = b.reshape(tiles, SUB, width)
    row = lax.broadcasted_iota(jnp.int32, a.shape, 1)
    for step in (1, 2, 4):
        shift = SUB - step if reverse else step
        inside = row < SUB - step if reverse else row >= step
        a_from = jnp.where(inside, pltpu.roll(a, shift, 1), 1.0)
        b_from = jnp.where(inside, pltpu.roll(b, shift, 1), 0.0)
        b = b + a * b_from
        a = a * a_from
    prod = jnp.ones((1, width), F32)
    state = jnp.zeros((1, width), F32)
    edge = 0 if reverse else SUB - 1
    for tile in reversed(range(tiles)) if reverse else range(tiles):
        here_b = b[tile] + a[tile] * state
        here_a = a[tile] * prod
        b_out[pl.ds(tile * SUB, SUB), :] = here_b
        a_out[pl.ds(tile * SUB, SUB), :] = here_a
        state = here_b[edge : edge + 1]
        prod = here_a[edge : edge + 1]
    return prod, state


def shift_up(value, last):
    rows = value.shape[0]
    row = lax.broadcasted_iota(jnp.int32, value.shape, 0)
    return jnp.where(row == rows - 1, last, pltpu.roll(value, rows - 1, 0))


def before_kernel(
    x_ref, prev_ref, rec_ref, inw_ref, cw_ref, cb_ref, ld_ref,
    decay_ref, beta_ref, conv_ref, cum_ref, local_ref, post_ref, slope_ref, ends_ref, front_ref,
    padded, scan_a, scan_b,
):
    rows = x_ref.shape[0]
    lead = prev_ref.shape[0]
    padded[pl.ds(0, lead), :] = prev_ref[...].astype(F32)
    padded[pl.ds(lead, rows), :] = x_ref[...].astype(F32)
    conv = jnp.zeros(x_ref.shape, F32)
    for lag in range(4):
        conv = conv + cw_ref[lag : lag + 1, :] * padded[pl.ds(lead - lag, rows), :]
    conv = cb_ref[...] + conv
    recur = sigmoid(rec_ref[...].astype(F32))
    inward = sigmoid(inw_ref[...].astype(F32))
    log_step = 8.0 * recur * ld_ref[...]
    decay = jnp.exp(log_step)
    beta = jnp.sqrt(-expm1(2.0 * log_step))
    decay_ref[...] = decay
    beta_ref[...] = beta
    conv_ref[...] = conv
    prod, state = local_scan(decay, beta * (inward * conv), False, cum_ref, local_ref)
    ends_ref[...] = jnp.concatenate([prod, state], axis=0)
    local_scan(decay, jnp.zeros_like(decay), True, scan_a, scan_b)
    post = shift_up(scan_a[...], 1.0)
    post_ref[...] = post
    slope = post * beta * inward
    slope_ref[...] = slope
    front_ref[...] = slope[:SUB]


def before(
    x_branch, prev, recurrence_gate, input_gate, conv_weight, conv_bias, log_decay
):
    rows, width = x_branch.shape
    full = jax.ShapeDtypeStruct((rows, width), F32)
    return pl.pallas_call(
        before_kernel,
        out_shape=(full,) * 7
        + (
            jax.ShapeDtypeStruct((2, width), F32),
            jax.ShapeDtypeStruct((SUB, width), F32),
        ),
        scratch_shapes=[
            pltpu.VMEM((rows + prev.shape[0], width), F32),
            pltpu.VMEM((rows, width), F32),
            pltpu.VMEM((rows, width), F32),
        ],
        compiler_params=pltpu.CompilerParams(vmem_limit_bytes=VMEM_LIMIT),
    )(x_branch, prev, recurrence_gate, input_gate, conv_weight, conv_bias, log_decay)


def adjoint_kernel(
    core_ref, own_ref, other_ref, w_ref, gate_ref, decay_ref, beta_ref, inw_ref, ends_ref,
    dlru_ref, adj_ref, offset_ref, front_ref, carry_ref,
    acc, scan_a, scan_b,
):
    step = pl.program_id(0)
    half = w_ref.shape[1] // 2

    @pl.when(step == 0)
    def _():
        acc[...] = jnp.zeros_like(acc)

    def add(first, second):
        dims = (((1,), (1,)), ((), ()))
        acc[...] += lax.dot_general(
            first, w_ref[:, :half], dims, preferred_element_type=F32
        ) + lax.dot_general(second, w_ref[:, half:], dims, preferred_element_type=F32)

    @pl.when(core_ref[0] == 0)
    def _():
        add(own_ref[0], other_ref[0])

    @pl.when(core_ref[0] != 0)
    def _():
        add(other_ref[0], own_ref[0])

    @pl.when(step == pl.num_programs(0) - 1)
    def _():
        d_lru = acc[...]
        dlru_ref[...] = d_lru
        d_direct = d_lru * gelu_parts(gate_ref[...].astype(F32))[0]
        decay = decay_ref[...]
        _, first = local_scan(decay, decay * d_direct, True, scan_a, scan_b)
        adj = d_direct + shift_up(scan_b[...], 0.0)
        adj_ref[...] = adj
        offset = adj * beta_ref[...] * sigmoid(inw_ref[...].astype(F32))
        offset_ref[...] = offset
        front_ref[...] = offset[:SUB]
        mine = jnp.concatenate([ends_ref[...], first], axis=0)
        carry_ref[...] = jnp.broadcast_to(mine[None], carry_ref.shape)


def adjoint(core, own, other, weights, gate, decay, beta, input_gate, ends, seq_count):
    rows, width = gate.shape
    steps = own.shape[0]
    full = jax.ShapeDtypeStruct((rows, width), F32)
    whole = lambda shape: pl.BlockSpec(shape, lambda i: (0,) * len(shape))
    return pl.pallas_call(
        adjoint_kernel,
        grid=(steps,),
        in_specs=[
            pl.BlockSpec(memory_space=pltpu.SMEM),
            pl.BlockSpec((1, rows, width), lambda i: (i, 0, 0)),
            pl.BlockSpec((1, rows, width), lambda i: (i, 0, 0)),
            pl.BlockSpec((width, 2 * width), lambda i: (0, i)),
            whole((rows, width)),
            whole((rows, width)),
            whole((rows, width)),
            whole((rows, width)),
            whole((2, width)),
        ],
        out_specs=[
            whole((rows, width)),
            whole((rows, width)),
            whole((rows, width)),
            whole((SUB, width)),
            whole((seq_count, 3, width)),
        ],
        out_shape=(
            full,
            full,
            full,
            jax.ShapeDtypeStruct((SUB, width), F32),
            jax.ShapeDtypeStruct((seq_count, 3, width), F32),
        ),
        scratch_shapes=[pltpu.VMEM((rows, width), F32)] * 3,
        compiler_params=pltpu.CompilerParams(vmem_limit_bytes=VMEM_WHOLE),
    )(core, own, other, weights, gate, decay, beta, input_gate, ends)


def branch_kernel(
    place_ref, carry_ref, offset_ref, slope_ref, cw_ref, front_a_ref, front_b_ref,
    branch_ref, kappa_ref,
    padded,
):
    rows, width = offset_ref.shape
    place = place_ref[0]
    beyond = jnp.zeros((1, width), F32)
    kappa = jnp.zeros((1, width), F32)
    for i in reversed(range(1, carry_ref.shape[0])):
        here = carry_ref[i, 2:3] + carry_ref[i, 0:1] * kappa
        beyond = jnp.where(i == place + 1, kappa, beyond)
        kappa = jnp.where(i > place, here, kappa)
    padded[pl.ds(0, rows), :] = offset_ref[...] + slope_ref[...] * kappa
    padded[pl.ds(rows, SUB), :] = front_a_ref[...] + front_b_ref[...] * beyond
    total = jnp.zeros((rows, width), F32)
    for lag in range(4):
        total = total + cw_ref[lag : lag + 1, :] * padded[pl.ds(lag, rows), :]
    branch_ref[...] = total.astype(BF16)
    kappa_ref[...] = kappa


def branch(place, carry, offset, slope, conv_weight, front_a, front_b):
    rows, width = offset.shape
    vmem = pl.BlockSpec(memory_space=pltpu.VMEM)
    return pl.pallas_call(
        branch_kernel,
        in_specs=[pl.BlockSpec(memory_space=pltpu.SMEM)] + [vmem] * 6,
        out_shape=(
            jax.ShapeDtypeStruct((rows, width), BF16),
            jax.ShapeDtypeStruct((1, width), F32),
        ),
        scratch_shapes=[pltpu.VMEM((rows + SUB, width), F32)],
        compiler_params=pltpu.CompilerParams(vmem_limit_bytes=VMEM_LIMIT),
    )(place, carry, offset, slope, conv_weight, front_a, front_b)


def gates_kernel(
    place_ref, carry_ref, kappa_ref, dlru_ref, adj_ref, post_ref, cum_ref, local_ref, decay_ref,
    beta_ref, conv_ref, gate_ref, rec_ref, inw_ref, ld_ref,
    dgate_ref, drec_ref, dinw_ref,
):
    place = place_ref[0]
    carried = jnp.zeros(kappa_ref.shape, F32)
    for i in range(carry_ref.shape[0] - 1):
        carried = jnp.where(i < place, carry_ref[i, 1:2] + carry_ref[i, 0:1] * carried, carried)
    states = local_ref[...] + cum_ref[...] * carried
    slope = gelu_parts(gate_ref[...].astype(F32))[1]
    dgate_ref[...] = (dlru_ref[...].astype(F32) * states * slope).astype(BF16)
    row = lax.broadcasted_iota(jnp.int32, states.shape, 0)
    states_prev = jnp.where(row == 0, carried, pltpu.roll(states, 1, 0))
    recur = sigmoid(rec_ref[...].astype(F32))
    inward = sigmoid(inw_ref[...].astype(F32))
    decay = decay_ref[...]
    beta = beta_ref[...]
    conv = conv_ref[...]
    adj = adj_ref[...] + post_ref[...] * kappa_ref[...]
    d_step = adj * (decay * states_prev - inward * conv * decay * decay / beta)
    drec_ref[...] = (d_step * 8.0 * ld_ref[...] * recur * (1.0 - recur)).astype(BF16)
    dinw_ref[...] = (adj * beta * conv * inward * (1.0 - inward)).astype(BF16)


def gates(place, carry, kappa, d_lru, *arrays):
    out = jax.ShapeDtypeStruct(d_lru.shape, BF16)
    vmem = pl.BlockSpec(memory_space=pltpu.VMEM)
    return pl.pallas_call(
        gates_kernel,
        in_specs=[pl.BlockSpec(memory_space=pltpu.SMEM)] + [vmem] * (3 + len(arrays)),
        out_shape=(out,) * 3,
        compiler_params=pltpu.CompilerParams(vmem_limit_bytes=VMEM_LIMIT),
    )(place, carry, kappa, d_lru, *arrays)


def input_kernel(core_ref, own_ref, other_ref, w_ref, out_ref, acc):
    step = pl.program_id(0)
    half = w_ref.shape[1] // 2

    @pl.when(step == 0)
    def _():
        acc[...] = jnp.zeros_like(acc)

    def add(first, second):
        dims = (((1,), (1,)), ((), ()))
        acc[...] += lax.dot_general(
            first, w_ref[:, :half], dims, preferred_element_type=F32
        ) + lax.dot_general(second, w_ref[:, half:], dims, preferred_element_type=F32)

    @pl.when(core_ref[0] == 0)
    def _():
        add(own_ref[0], other_ref[0])

    @pl.when(core_ref[0] != 0)
    def _():
        add(other_ref[0], own_ref[0])

    @pl.when(step == pl.num_programs(0) - 1)
    def _():
        out_ref[...] = acc[...].astype(BF16)


def input_grad(core, own, other, weights):
    steps, rows, width = own.shape
    return pl.pallas_call(
        input_kernel,
        grid=(steps,),
        in_specs=[
            pl.BlockSpec(memory_space=pltpu.SMEM),
            pl.BlockSpec((1, rows, width), lambda i: (i, 0, 0)),
            pl.BlockSpec((1, rows, width), lambda i: (i, 0, 0)),
            pl.BlockSpec((weights.shape[0], 2 * width), lambda i: (0, i)),
        ],
        out_specs=pl.BlockSpec((rows, weights.shape[0]), lambda i: (0, 0)),
        out_shape=jax.ShapeDtypeStruct((rows, weights.shape[0]), BF16),
        scratch_shapes=[pltpu.VMEM((rows, weights.shape[0]), F32)],
        compiler_params=pltpu.CompilerParams(vmem_limit_bytes=VMEM_WHOLE),
    )(core, own, other, weights)


def shards(
    d_out,
    x_branch,
    gate_branch,
    recurrence_gate,
    input_gate,
    conv_weight,
    conv_bias,
    decay_level,
    w_in,
    w_out,
):
    tok_rows, width = x_branch.shape
    seq_count = lax.axis_size(SEQ)
    place = lax.axis_index(SEQ).astype(jnp.int32).reshape(1)
    core = lax.axis_index("k").astype(jnp.int32).reshape(1)
    forward = [(i, i + 1) for i in range(seq_count - 1)]
    backward = [(i + 1, i) for i in range(seq_count - 1)]
    cores = [(0, 1), (1, 0)]

    spread = jnp.broadcast_to(w_out[None], (lax.axis_size("y"),) + w_out.shape)
    out_part = lax.all_to_all(spread, "y", 0, 0).reshape(-1, w_out.shape[1])
    out_part, w_in = lax.optimization_barrier((out_part, w_in))
    out_rows = lax.all_gather(out_part, "z", axis=0, tiled=True)
    in_part = lax.all_gather(w_in, "y", axis=0, tiled=True)
    in_rows = lax.all_gather(in_part, "z", axis=0, tiled=True)
    out_own = lax.all_gather(d_out, "x")
    out_other = lax.ppermute(out_own, "k", cores)
    prev = lax.ppermute(x_branch[tok_rows - 16 :], SEQ, forward)
    log_table = decay_table(tok_rows * seq_count)
    onehot = decay_level[:, None] == jnp.arange(LEVELS)[None, :]
    log_decay = jnp.sum(jnp.where(onehot, log_table[None, :], 0.0), axis=1)[None, :]
    decay, beta, conv_out, cum_decay, local_states, post, slope, ends, front_b = before(
        x_branch, prev, recurrence_gate, input_gate, conv_weight, conv_bias[None, :], log_decay
    )

    next_b = lax.ppermute(front_b, SEQ, backward)

    ends, next_b, in_part = lax.optimization_barrier((ends, next_b, in_part))
    d_lru, adj_local, offset, front_a, carry = adjoint(
        core, out_own, out_other, out_rows, gate_branch, decay, beta, input_gate, ends, seq_count
    )
    next_a = lax.ppermute(front_a, SEQ, backward)
    carries = lax.all_to_all(carry, SEQ, 0, 0)
    d_branch, kappa = branch(place, carries, offset, slope, conv_weight, next_a, next_b)
    own = lax.all_gather(d_branch, "x")
    other = lax.ppermute(own, "k", cores)
    d_gate, d_recurrence_gate, d_input_gate = gates(
        place, carries, kappa, d_lru, adj_local, post, cum_decay, local_states, decay,
        beta, conv_out, gate_branch, recurrence_gate, input_gate, log_decay,
    )
    d_input = input_grad(core, own, other, in_rows)
    return (d_input, d_gate, d_recurrence_gate, d_input_gate)


def solution(mesh):
    fine = Mesh(mesh.devices.reshape(8, 8, 4, 2), SEQ + CHAN)
    tokens = P(SEQ, CHAN)
    rows = P(CHAN + SEQ, None)
    in_specs = (tokens,) * 5 + (P(None, CHAN), P(CHAN), P(CHAN), rows, rows)
    return jax.shard_map(
        shards, mesh=fine, in_specs=in_specs, out_specs=(tokens,) * 4, check_vma=False
    )
```

```python
import functools

import jax
import jax.numpy as jnp
from jax import lax
from jax.experimental import pallas as pl
from jax.experimental.pallas import tpu as pltpu
from jax.sharding import Mesh, PartitionSpec as P

LEVELS = 16
SEQ = ("z", "y")
CHAN = ("x", "k")
SUB = 8
F32 = jnp.float32
BF16 = jnp.bfloat16
VMEM_LIMIT = 24 * 1024 * 1024
VMEM_WHOLE = 61 * 1024 * 1024


def decay_table(length):
    levels = jnp.arange(LEVELS).astype(F32)
    half = LEVELS // 2
    slow_rates = 0.25 * jnp.power(16.0, levels / (half - 1.0)) / (8.0 * length)
    fast_rates = jnp.power(4.0, (levels - half) / (half - 1.0)) / 640.0
    return -jnp.where(levels < half, slow_rates, fast_rates)


def gelu_parts(gate):
    normal_cdf = 0.5 * (1.0 + lax.erf(gate * 0.7071067811865476))
    density = jnp.exp(-0.5 * gate * gate) * 0.3989422804014327
    return (gate * normal_cdf, normal_cdf + gate * density)


def sigmoid(value):
    return 1.0 / (1.0 + jnp.exp(-value))


def expm1(value):
    series = jnp.ones_like(value)
    for term in range(9, 1, -1):
        series = 1.0 + value * (1.0 / term) * series
    return jnp.where(jnp.abs(value) < 0.5, value * series, jnp.exp(value) - 1.0)


def local_scan(a, b, reverse, a_out, b_out):
    rows, width = a.shape
    tiles = rows // SUB
    a = a.reshape(tiles, SUB, width)
    b = b.reshape(tiles, SUB, width)
    row = lax.broadcasted_iota(jnp.int32, a.shape, 1)
    for step in (1, 2, 4):
        shift = SUB - step if reverse else step
        inside = row < SUB - step if reverse else row >= step
        a_from = jnp.where(inside, pltpu.roll(a, shift, 1), 1.0)
        b_from = jnp.where(inside, pltpu.roll(b, shift, 1), 0.0)
        b = b + a * b_from
        a = a * a_from
    prod = jnp.ones((1, width), F32)
    state = jnp.zeros((1, width), F32)
    edge = 0 if reverse else SUB - 1
    for tile in reversed(range(tiles)) if reverse else range(tiles):
        here_b = b[tile] + a[tile] * state
        here_a = a[tile] * prod
        b_out[pl.ds(tile * SUB, SUB), :] = here_b
        a_out[pl.ds(tile * SUB, SUB), :] = here_a
        state = here_b[edge : edge + 1]
        prod = here_a[edge : edge + 1]
    return prod, state


def shift_up(value, last):
    rows = value.shape[0]
    row = lax.broadcasted_iota(jnp.int32, value.shape, 0)
    return jnp.where(row == rows - 1, last, pltpu.roll(value, rows - 1, 0))


def before_kernel(
    x_ref, prev_ref, rec_ref, inw_ref, cw_ref, cb_ref, ld_ref,
    decay_ref, beta_ref, conv_ref, cum_ref, local_ref, post_ref, slope_ref, ends_ref, front_ref,
    padded, scan_a, scan_b,
):
    rows = x_ref.shape[0]
    lead = prev_ref.shape[0]
    padded[pl.ds(0, lead), :] = prev_ref[...].astype(F32)
    padded[pl.ds(lead, rows), :] = x_ref[...].astype(F32)
    conv = jnp.zeros(x_ref.shape, F32)
    for lag in range(4):
        conv = conv + cw_ref[lag : lag + 1, :] * padded[pl.ds(lead - lag, rows), :]
    conv = cb_ref[...] + conv
    recur = sigmoid(rec_ref[...].astype(F32))
    inward = sigmoid(inw_ref[...].astype(F32))
    log_step = 8.0 * recur * ld_ref[...]
    decay = jnp.exp(log_step)
    beta = jnp.sqrt(-expm1(2.0 * log_step))
    decay_ref[...] = decay
    beta_ref[...] = beta
    conv_ref[...] = conv
    prod, state = local_scan(decay, beta * (inward * conv), False, cum_ref, local_ref)
    ends = jnp.concatenate([prod, state], axis=0)
    ends_ref[...] = jnp.broadcast_to(ends[None], ends_ref.shape)
    local_scan(decay, jnp.zeros_like(decay), True, scan_a, scan_b)
    post = shift_up(scan_a[...], 1.0)
    post_ref[...] = post
    slope = post * beta * inward
    slope_ref[...] = slope
    front_ref[...] = slope[:SUB]


def before(
    x_branch, prev, recurrence_gate, input_gate, conv_weight, conv_bias, log_decay, seq_count
):
    rows, width = x_branch.shape
    full = jax.ShapeDtypeStruct((rows, width), F32)
    return pl.pallas_call(
        before_kernel,
        out_shape=(full,) * 7
        + (
            jax.ShapeDtypeStruct((seq_count, 2, width), F32),
            jax.ShapeDtypeStruct((SUB, width), F32),
        ),
        scratch_shapes=[
            pltpu.VMEM((rows + prev.shape[0], width), F32),
            pltpu.VMEM((rows, width), F32),
            pltpu.VMEM((rows, width), F32),
        ],
        compiler_params=pltpu.CompilerParams(vmem_limit_bytes=VMEM_LIMIT),
    )(x_branch, prev, recurrence_gate, input_gate, conv_weight, conv_bias, log_decay)


def adjoint_kernel(
    core_ref, own_ref, other_ref, w_ref, gate_ref, decay_ref, beta_ref, inw_ref,
    dlru_ref, adj_ref, offset_ref, front_ref, edge_ref,
    acc, scan_a, scan_b,
):
    step = pl.program_id(0)
    half = w_ref.shape[1] // 2

    @pl.when(step == 0)
    def _():
        acc[...] = jnp.zeros_like(acc)

    def add(first, second):
        dims = (((1,), (1,)), ((), ()))
        acc[...] += lax.dot_general(
            first, w_ref[:, :half], dims, preferred_element_type=F32
        ) + lax.dot_general(second, w_ref[:, half:], dims, preferred_element_type=F32)

    @pl.when(core_ref[0] == 0)
    def _():
        add(own_ref[0], other_ref[0])

    @pl.when(core_ref[0] != 0)
    def _():
        add(other_ref[0], own_ref[0])

    @pl.when(step == pl.num_programs(0) - 1)
    def _():
        d_lru = acc[...]
        dlru_ref[...] = d_lru
        d_direct = d_lru * gelu_parts(gate_ref[...].astype(F32))[0]
        decay = decay_ref[...]
        _, first = local_scan(decay, decay * d_direct, True, scan_a, scan_b)
        adj = d_direct + shift_up(scan_b[...], 0.0)
        adj_ref[...] = adj
        offset = adj * beta_ref[...] * sigmoid(inw_ref[...].astype(F32))
        offset_ref[...] = offset
        front_ref[...] = offset[:SUB]
        edge_ref[...] = jnp.broadcast_to(first[None], edge_ref.shape)


def adjoint(core, own, other, weights, gate, decay, beta, input_gate, seq_count):
    rows, width = gate.shape
    steps = own.shape[0]
    full = jax.ShapeDtypeStruct((rows, width), F32)
    whole = lambda shape: pl.BlockSpec(shape, lambda i: (0,) * len(shape))
    return pl.pallas_call(
        adjoint_kernel,
        grid=(steps,),
        in_specs=[
            pl.BlockSpec(memory_space=pltpu.SMEM),
            pl.BlockSpec((1, rows, width), lambda i: (i, 0, 0)),
            pl.BlockSpec((1, rows, width), lambda i: (i, 0, 0)),
            pl.BlockSpec((width, 2 * width), lambda i: (0, i)),
            whole((rows, width)),
            whole((rows, width)),
            whole((rows, width)),
            whole((rows, width)),
        ],
        out_specs=[
            whole((rows, width)),
            whole((rows, width)),
            whole((rows, width)),
            whole((SUB, width)),
            whole((seq_count, 1, width)),
        ],
        out_shape=(
            full,
            full,
            full,
            jax.ShapeDtypeStruct((SUB, width), F32),
            jax.ShapeDtypeStruct((seq_count, 1, width), F32),
        ),
        scratch_shapes=[pltpu.VMEM((rows, width), F32)] * 3,
        compiler_params=pltpu.CompilerParams(vmem_limit_bytes=VMEM_WHOLE),
    )(core, own, other, weights, gate, decay, beta, input_gate)


def branch_kernel(
    place_ref, ends_ref, edge_ref, offset_ref, slope_ref, cw_ref, front_a_ref, front_b_ref,
    branch_ref, kappa_ref,
    padded,
):
    rows, width = offset_ref.shape
    place = place_ref[0]
    beyond = jnp.zeros((1, width), F32)
    kappa = jnp.zeros((1, width), F32)
    for i in reversed(range(1, ends_ref.shape[0])):
        here = edge_ref[i] + ends_ref[i, 0:1] * kappa
        beyond = jnp.where(i == place + 1, kappa, beyond)
        kappa = jnp.where(i > place, here, kappa)
    padded[pl.ds(0, rows), :] = offset_ref[...] + slope_ref[...] * kappa
    padded[pl.ds(rows, SUB), :] = front_a_ref[...] + front_b_ref[...] * beyond
    total = jnp.zeros((rows, width), F32)
    for lag in range(4):
        total = total + cw_ref[lag : lag + 1, :] * padded[pl.ds(lag, rows), :]
    branch_ref[...] = total.astype(BF16)
    kappa_ref[...] = kappa


def branch(place, ends, edges, offset, slope, conv_weight, front_a, front_b):
    rows, width = offset.shape
    vmem = pl.BlockSpec(memory_space=pltpu.VMEM)
    return pl.pallas_call(
        branch_kernel,
        in_specs=[pl.BlockSpec(memory_space=pltpu.SMEM)] + [vmem] * 7,
        out_shape=(
            jax.ShapeDtypeStruct((rows, width), BF16),
            jax.ShapeDtypeStruct((1, width), F32),
        ),
        scratch_shapes=[pltpu.VMEM((rows + SUB, width), F32)],
        compiler_params=pltpu.CompilerParams(vmem_limit_bytes=VMEM_LIMIT),
    )(place, ends, edges, offset, slope, conv_weight, front_a, front_b)


def gates_kernel(
    place_ref, carry_ref, kappa_ref, dlru_ref, adj_ref, post_ref, cum_ref, local_ref, decay_ref,
    beta_ref, conv_ref, gate_ref, rec_ref, inw_ref, ld_ref,
    dgate_ref, drec_ref, dinw_ref,
):
    place = place_ref[0]
    carried = jnp.zeros(kappa_ref.shape, F32)
    for i in range(carry_ref.shape[0] - 1):
        carried = jnp.where(i < place, carry_ref[i, 1:2] + carry_ref[i, 0:1] * carried, carried)
    states = local_ref[...] + cum_ref[...] * carried
    slope = gelu_parts(gate_ref[...].astype(F32))[1]
    dgate_ref[...] = (dlru_ref[...].astype(F32) * states * slope).astype(BF16)
    row = lax.broadcasted_iota(jnp.int32, states.shape, 0)
    states_prev = jnp.where(row == 0, carried, pltpu.roll(states, 1, 0))
    recur = sigmoid(rec_ref[...].astype(F32))
    inward = sigmoid(inw_ref[...].astype(F32))
    decay = decay_ref[...]
    beta = beta_ref[...]
    conv = conv_ref[...]
    adj = adj_ref[...] + post_ref[...] * kappa_ref[...]
    d_step = adj * (decay * states_prev - inward * conv * decay * decay / beta)
    drec_ref[...] = (d_step * 8.0 * ld_ref[...] * recur * (1.0 - recur)).astype(BF16)
    dinw_ref[...] = (adj * beta * conv * inward * (1.0 - inward)).astype(BF16)


def gates(place, carry, kappa, d_lru, *arrays):
    out = jax.ShapeDtypeStruct(d_lru.shape, BF16)
    vmem = pl.BlockSpec(memory_space=pltpu.VMEM)
    return pl.pallas_call(
        gates_kernel,
        in_specs=[pl.BlockSpec(memory_space=pltpu.SMEM)] + [vmem] * (3 + len(arrays)),
        out_shape=(out,) * 3,
        compiler_params=pltpu.CompilerParams(vmem_limit_bytes=VMEM_LIMIT),
    )(place, carry, kappa, d_lru, *arrays)


def input_kernel(lead, core_ref, own_ref, other_ref, first_ref, rest_ref, out_ref, acc):
    step = pl.program_id(0)
    half = first_ref.shape[1] // 2

    @pl.when(step == 0)
    def _():
        acc[...] = jnp.zeros_like(acc)

    def product(left, right, w_ref):
        dims = (((1,), (1,)), ((), ()))
        return lax.dot_general(
            left, w_ref[:, :half], dims, preferred_element_type=F32
        ) + lax.dot_general(right, w_ref[:, half:], dims, preferred_element_type=F32)

    def add(left, right):
        @pl.when(step < lead)
        def _():
            acc[...] += product(left[0], right[0], first_ref)

        @pl.when(step >= lead)
        def _():
            acc[...] += product(left[0], right[0], rest_ref)

    @pl.when(core_ref[0] == 0)
    def _():
        add(own_ref, other_ref)

    @pl.when(core_ref[0] != 0)
    def _():
        add(other_ref, own_ref)

    @pl.when(step == pl.num_programs(0) - 1)
    def _():
        out_ref[...] = acc[...].astype(BF16)


def input_grad(core, own, other, first, rest):
    steps, rows, width = own.shape
    feats = first.shape[0]
    lead = steps - rest.shape[1] // (2 * width)
    at = first.shape[1] // (2 * width) - lead
    return pl.pallas_call(
        functools.partial(input_kernel, lead),
        grid=(steps,),
        in_specs=[
            pl.BlockSpec(memory_space=pltpu.SMEM),
            pl.BlockSpec((1, rows, width), lambda i: (i, 0, 0)),
            pl.BlockSpec((1, rows, width), lambda i: (i, 0, 0)),
            pl.BlockSpec((feats, 2 * width), lambda i: (0, at + jnp.minimum(i, lead - 1))),
            pl.BlockSpec((feats, 2 * width), lambda i: (0, jnp.maximum(i - lead, 0))),
        ],
        out_specs=pl.BlockSpec((rows, feats), lambda i: (0, 0)),
        out_shape=jax.ShapeDtypeStruct((rows, feats), BF16),
        scratch_shapes=[pltpu.VMEM((rows, feats), F32)],
        compiler_params=pltpu.CompilerParams(vmem_limit_bytes=VMEM_WHOLE),
    )(core, own, other, first, rest)


def shards(
    d_out,
    x_branch,
    gate_branch,
    recurrence_gate,
    input_gate,
    conv_weight,
    conv_bias,
    decay_level,
    w_in,
    w_out,
):
    tok_rows, width = x_branch.shape
    seq_count = lax.axis_size(SEQ)
    place = lax.axis_index(SEQ).astype(jnp.int32).reshape(1)
    core = lax.axis_index("k").astype(jnp.int32).reshape(1)
    forward = [(i, i + 1) for i in range(seq_count - 1)]
    backward = [(i + 1, i) for i in range(seq_count - 1)]
    cores = [(0, 1), (1, 0)]

    half = w_in.shape[1] // 2
    first = jnp.concatenate([w_out, w_in[:, :half]], axis=1)
    first = lax.all_gather(first, SEQ, axis=0, tiled=True)
    rest = lax.all_gather(w_in[:, half:], "y", axis=0, tiled=True)
    in_rows = lax.all_gather(rest, "z", axis=0, tiled=True)
    out_own = lax.all_gather(d_out, "x")
    out_other = lax.ppermute(out_own, "k", cores)
    prev = lax.ppermute(x_branch[tok_rows - 16 :], SEQ, forward)
    log_table = decay_table(tok_rows * seq_count)
    onehot = decay_level[:, None] == jnp.arange(LEVELS)[None, :]
    log_decay = jnp.sum(jnp.where(onehot, log_table[None, :], 0.0), axis=1)[None, :]
    decay, beta, conv_out, cum_decay, local_states, post, slope, ends, front_b = before(
        x_branch, prev, recurrence_gate, input_gate, conv_weight, conv_bias[None, :], log_decay,
        seq_count,
    )

    next_b = lax.ppermute(front_b, SEQ, backward)

    all_ends = lax.all_to_all(ends, SEQ, 0, 0)
    decay, all_ends, next_b = lax.optimization_barrier((decay, all_ends, next_b))
    d_lru, adj_local, offset, front_a, edge = adjoint(
        core, out_own, out_other, first, gate_branch, decay, beta, input_gate, seq_count
    )
    next_a = lax.ppermute(front_a, SEQ, backward)
    edges = lax.all_to_all(edge, SEQ, 0, 0)
    d_branch, kappa = branch(place, all_ends, edges, offset, slope, conv_weight, next_a, next_b)
    own = lax.all_gather(d_branch, "x")
    other = lax.ppermute(own, "k", cores)
    d_gate, d_recurrence_gate, d_input_gate = gates(
        place, all_ends, kappa, d_lru, adj_local, post, cum_decay, local_states, decay,
        beta, conv_out, gate_branch, recurrence_gate, input_gate, log_decay,
    )
    d_input = input_grad(core, own, other, first, in_rows)
    return (d_input, d_gate, d_recurrence_gate, d_input_gate)


def solution(mesh):
    fine = Mesh(mesh.devices.reshape(8, 8, 4, 2), SEQ + CHAN)
    tokens = P(SEQ, CHAN)
    rows = P(CHAN + SEQ, None)
    in_specs = (tokens,) * 5 + (P(None, CHAN), P(CHAN), P(CHAN), rows, rows)
    return jax.shard_map(
        shards, mesh=fine, in_specs=in_specs, out_specs=(tokens,) * 4, check_vma=False
    )
```

```python
import jax
import jax.numpy as jnp
from jax import lax
from jax.experimental import pallas as pl
from jax.experimental.pallas import tpu as pltpu
from jax.sharding import Mesh, PartitionSpec as P

LEVELS = 16
SEQ = ("z", "y")
CHAN = ("x", "k")
SUB = 8
F32 = jnp.float32
BF16 = jnp.bfloat16
VMEM_LIMIT = 24 * 1024 * 1024
VMEM_WHOLE = 61 * 1024 * 1024


def decay_table(length):
    levels = jnp.arange(LEVELS).astype(F32)
    half = LEVELS // 2
    slow_rates = 0.25 * jnp.power(16.0, levels / (half - 1.0)) / (8.0 * length)
    fast_rates = jnp.power(4.0, (levels - half) / (half - 1.0)) / 640.0
    return -jnp.where(levels < half, slow_rates, fast_rates)


def gelu_parts(gate):
    normal_cdf = 0.5 * (1.0 + lax.erf(gate * 0.7071067811865476))
    density = jnp.exp(-0.5 * gate * gate) * 0.3989422804014327
    return (gate * normal_cdf, normal_cdf + gate * density)


def sigmoid(value):
    return 1.0 / (1.0 + jnp.exp(-value))


def expm1(value):
    series = jnp.ones_like(value)
    for term in range(9, 1, -1):
        series = 1.0 + value * (1.0 / term) * series
    return jnp.where(jnp.abs(value) < 0.5, value * series, jnp.exp(value) - 1.0)


def local_scan(a, b, reverse, a_out, b_out):
    rows, width = a.shape
    tiles = rows // SUB
    a = a.reshape(tiles, SUB, width)
    b = b.reshape(tiles, SUB, width)
    row = lax.broadcasted_iota(jnp.int32, a.shape, 1)
    for step in (1, 2, 4):
        shift = SUB - step if reverse else step
        inside = row < SUB - step if reverse else row >= step
        a_from = jnp.where(inside, pltpu.roll(a, shift, 1), 1.0)
        b_from = jnp.where(inside, pltpu.roll(b, shift, 1), 0.0)
        b = b + a * b_from
        a = a * a_from
    prod = jnp.ones((1, width), F32)
    state = jnp.zeros((1, width), F32)
    edge = 0 if reverse else SUB - 1
    for tile in reversed(range(tiles)) if reverse else range(tiles):
        here_b = b[tile] + a[tile] * state
        here_a = a[tile] * prod
        b_out[pl.ds(tile * SUB, SUB), :] = here_b
        a_out[pl.ds(tile * SUB, SUB), :] = here_a
        state = here_b[edge : edge + 1]
        prod = here_a[edge : edge + 1]
    return prod, state


def shift_up(value, last):
    rows = value.shape[0]
    row = lax.broadcasted_iota(jnp.int32, value.shape, 0)
    return jnp.where(row == rows - 1, last, pltpu.roll(value, rows - 1, 0))


def before_kernel(
    x_ref, prev_ref, rec_ref, inw_ref, cw_ref, cb_ref, ld_ref,
    decay_ref, beta_ref, conv_ref, cum_ref, local_ref, post_ref, slope_ref, ends_ref, front_ref,
    padded, scan_a, scan_b,
):
    rows = x_ref.shape[0]
    lead = prev_ref.shape[0]
    padded[pl.ds(0, lead), :] = prev_ref[...].astype(F32)
    padded[pl.ds(lead, rows), :] = x_ref[...].astype(F32)
    conv = jnp.zeros(x_ref.shape, F32)
    for lag in range(4):
        conv = conv + cw_ref[lag : lag + 1, :] * padded[pl.ds(lead - lag, rows), :]
    conv = cb_ref[...] + conv
    recur = sigmoid(rec_ref[...].astype(F32))
    inward = sigmoid(inw_ref[...].astype(F32))
    log_step = 8.0 * recur * ld_ref[...]
    decay = jnp.exp(log_step)
    beta = jnp.sqrt(-expm1(2.0 * log_step))
    decay_ref[...] = decay
    beta_ref[...] = beta
    conv_ref[...] = conv
    prod, state = local_scan(decay, beta * (inward * conv), False, cum_ref, local_ref)
    ends_ref[...] = jnp.concatenate([prod, state], axis=0)
    local_scan(decay, jnp.zeros_like(decay), True, scan_a, scan_b)
    post = shift_up(scan_a[...], 1.0)
    post_ref[...] = post
    slope = post * beta * inward
    slope_ref[...] = slope
    front_ref[...] = slope[:SUB]


def before(
    x_branch, prev, recurrence_gate, input_gate, conv_weight, conv_bias, log_decay
):
    rows, width = x_branch.shape
    full = jax.ShapeDtypeStruct((rows, width), F32)
    return pl.pallas_call(
        before_kernel,
        out_shape=(full,) * 7
        + (
            jax.ShapeDtypeStruct((2, width), F32),
            jax.ShapeDtypeStruct((SUB, width), F32),
        ),
        scratch_shapes=[
            pltpu.VMEM((rows + prev.shape[0], width), F32),
            pltpu.VMEM((rows, width), F32),
            pltpu.VMEM((rows, width), F32),
        ],
        compiler_params=pltpu.CompilerParams(vmem_limit_bytes=VMEM_LIMIT),
    )(x_branch, prev, recurrence_gate, input_gate, conv_weight, conv_bias, log_decay)


def adjoint_kernel(
    core_ref, own_ref, other_ref, w_ref, gate_ref, decay_ref, beta_ref, inw_ref, ends_ref,
    dlru_ref, adj_ref, offset_ref, front_ref, carry_ref,
    acc, scan_a, scan_b,
):
    step = pl.program_id(0)
    half = w_ref.shape[1] // 2

    @pl.when(step == 0)
    def _():
        acc[...] = jnp.zeros_like(acc)

    def add(first, second):
        dims = (((1,), (1,)), ((), ()))
        acc[...] += lax.dot_general(
            first, w_ref[:, :half], dims, preferred_element_type=F32
        ) + lax.dot_general(second, w_ref[:, half:], dims, preferred_element_type=F32)

    @pl.when(core_ref[0] == 0)
    def _():
        add(own_ref[0], other_ref[0])

    @pl.when(core_ref[0] != 0)
    def _():
        add(other_ref[0], own_ref[0])

    @pl.when(step == pl.num_programs(0) - 1)
    def _():
        d_lru = acc[...]
        dlru_ref[...] = d_lru
        d_direct = d_lru * gelu_parts(gate_ref[...].astype(F32))[0]
        decay = decay_ref[...]
        _, first = local_scan(decay, decay * d_direct, True, scan_a, scan_b)
        adj = d_direct + shift_up(scan_b[...], 0.0)
        adj_ref[...] = adj
        offset = adj * beta_ref[...] * sigmoid(inw_ref[...].astype(F32))
        offset_ref[...] = offset
        front_ref[...] = offset[:SUB]
        mine = jnp.concatenate([ends_ref[...], first], axis=0)
        carry_ref[...] = jnp.broadcast_to(mine[None], carry_ref.shape)


def adjoint(core, own, other, weights, gate, decay, beta, input_gate, ends, seq_count):
    rows, width = gate.shape
    steps = own.shape[0]
    full = jax.ShapeDtypeStruct((rows, width), F32)
    whole = lambda shape: pl.BlockSpec(shape, lambda i: (0,) * len(shape))
    return pl.pallas_call(
        adjoint_kernel,
        grid=(steps,),
        in_specs=[
            pl.BlockSpec(memory_space=pltpu.SMEM),
            pl.BlockSpec((1, rows, width), lambda i: (i, 0, 0)),
            pl.BlockSpec((1, rows, width), lambda i: (i, 0, 0)),
            pl.BlockSpec((width, 2 * width), lambda i: (0, i)),
            whole((rows, width)),
            whole((rows, width)),
            whole((rows, width)),
            whole((rows, width)),
            whole((2, width)),
        ],
        out_specs=[
            whole((rows, width)),
            whole((rows, width)),
            whole((rows, width)),
            whole((SUB, width)),
            whole((seq_count, 3, width)),
        ],
        out_shape=(
            full,
            full,
            full,
            jax.ShapeDtypeStruct((SUB, width), F32),
            jax.ShapeDtypeStruct((seq_count, 3, width), F32),
        ),
        scratch_shapes=[pltpu.VMEM((rows, width), F32)] * 3,
        compiler_params=pltpu.CompilerParams(vmem_limit_bytes=VMEM_WHOLE),
    )(core, own, other, weights, gate, decay, beta, input_gate, ends)


def branch_kernel(
    place_ref, carry_ref, offset_ref, slope_ref, cw_ref, front_a_ref, front_b_ref,
    branch_ref, kappa_ref,
    padded,
):
    rows, width = offset_ref.shape
    place = place_ref[0]
    beyond = jnp.zeros((1, width), F32)
    kappa = jnp.zeros((1, width), F32)
    for i in reversed(range(1, carry_ref.shape[0])):
        here = carry_ref[i, 2:3] + carry_ref[i, 0:1] * kappa
        beyond = jnp.where(i == place + 1, kappa, beyond)
        kappa = jnp.where(i > place, here, kappa)
    padded[pl.ds(0, rows), :] = offset_ref[...] + slope_ref[...] * kappa
    padded[pl.ds(rows, SUB), :] = front_a_ref[...] + front_b_ref[...] * beyond
    total = jnp.zeros((rows, width), F32)
    for lag in range(4):
        total = total + cw_ref[lag : lag + 1, :] * padded[pl.ds(lag, rows), :]
    branch_ref[...] = total.astype(BF16)
    kappa_ref[...] = kappa


def branch(place, carry, offset, slope, conv_weight, front_a, front_b):
    rows, width = offset.shape
    vmem = pl.BlockSpec(memory_space=pltpu.VMEM)
    return pl.pallas_call(
        branch_kernel,
        in_specs=[pl.BlockSpec(memory_space=pltpu.SMEM)] + [vmem] * 6,
        out_shape=(
            jax.ShapeDtypeStruct((rows, width), BF16),
            jax.ShapeDtypeStruct((1, width), F32),
        ),
        scratch_shapes=[pltpu.VMEM((rows + SUB, width), F32)],
        compiler_params=pltpu.CompilerParams(vmem_limit_bytes=VMEM_LIMIT),
    )(place, carry, offset, slope, conv_weight, front_a, front_b)


def gates_kernel(
    place_ref, carry_ref, kappa_ref, dlru_ref, adj_ref, post_ref, cum_ref, local_ref, decay_ref,
    beta_ref, conv_ref, gate_ref, rec_ref, inw_ref, ld_ref,
    dgate_ref, drec_ref, dinw_ref,
):
    place = place_ref[0]
    carried = jnp.zeros(kappa_ref.shape, F32)
    for i in range(carry_ref.shape[0] - 1):
        carried = jnp.where(i < place, carry_ref[i, 1:2] + carry_ref[i, 0:1] * carried, carried)
    states = local_ref[...] + cum_ref[...] * carried
    slope = gelu_parts(gate_ref[...].astype(F32))[1]
    dgate_ref[...] = (dlru_ref[...].astype(F32) * states * slope).astype(BF16)
    row = lax.broadcasted_iota(jnp.int32, states.shape, 0)
    states_prev = jnp.where(row == 0, carried, pltpu.roll(states, 1, 0))
    recur = sigmoid(rec_ref[...].astype(F32))
    inward = sigmoid(inw_ref[...].astype(F32))
    decay = decay_ref[...]
    beta = beta_ref[...]
    conv = conv_ref[...]
    adj = adj_ref[...] + post_ref[...] * kappa_ref[...]
    d_step = adj * (decay * states_prev - inward * conv * decay * decay / beta)
    drec_ref[...] = (d_step * 8.0 * ld_ref[...] * recur * (1.0 - recur)).astype(BF16)
    dinw_ref[...] = (adj * beta * conv * inward * (1.0 - inward)).astype(BF16)


def gates(place, carry, kappa, d_lru, *arrays):
    out = jax.ShapeDtypeStruct(d_lru.shape, BF16)
    vmem = pl.BlockSpec(memory_space=pltpu.VMEM)
    return pl.pallas_call(
        gates_kernel,
        in_specs=[pl.BlockSpec(memory_space=pltpu.SMEM)] + [vmem] * (3 + len(arrays)),
        out_shape=(out,) * 3,
        compiler_params=pltpu.CompilerParams(vmem_limit_bytes=VMEM_LIMIT),
    )(place, carry, kappa, d_lru, *arrays)


def input_kernel(core_ref, own_ref, other_ref, w_ref, out_ref, acc):
    step = pl.program_id(0)
    half = w_ref.shape[1] // 2

    @pl.when(step == 0)
    def _():
        acc[...] = jnp.zeros_like(acc)

    def add(first, second):
        dims = (((1,), (1,)), ((), ()))
        acc[...] += lax.dot_general(
            w_ref[:, :half], first, dims, preferred_element_type=F32
        ) + lax.dot_general(w_ref[:, half:], second, dims, preferred_element_type=F32)

    @pl.when(core_ref[0] == 0)
    def _():
        add(own_ref[0], other_ref[0])

    @pl.when(core_ref[0] != 0)
    def _():
        add(other_ref[0], own_ref[0])

    @pl.when(step == pl.num_programs(0) - 1)
    def _():
        out_ref[...] = acc[...].T.astype(BF16)


def input_grad(core, own, other, weights):
    steps, rows, width = own.shape
    return pl.pallas_call(
        input_kernel,
        grid=(steps,),
        in_specs=[
            pl.BlockSpec(memory_space=pltpu.SMEM),
            pl.BlockSpec((1, rows, width), lambda i: (i, 0, 0)),
            pl.BlockSpec((1, rows, width), lambda i: (i, 0, 0)),
            pl.BlockSpec((weights.shape[0], 2 * width), lambda i: (0, i)),
        ],
        out_specs=pl.BlockSpec((rows, weights.shape[0]), lambda i: (0, 0)),
        out_shape=jax.ShapeDtypeStruct((rows, weights.shape[0]), BF16),
        scratch_shapes=[pltpu.VMEM((weights.shape[0], rows), F32)],
        compiler_params=pltpu.CompilerParams(vmem_limit_bytes=VMEM_WHOLE),
    )(core, own, other, weights)


def shards(
    d_out,
    x_branch,
    gate_branch,
    recurrence_gate,
    input_gate,
    conv_weight,
    conv_bias,
    decay_level,
    w_in,
    w_out,
):
    tok_rows, width = x_branch.shape
    seq_count = lax.axis_size(SEQ)
    place = lax.axis_index(SEQ).astype(jnp.int32).reshape(1)
    core = lax.axis_index("k").astype(jnp.int32).reshape(1)
    forward = [(i, i + 1) for i in range(seq_count - 1)]
    backward = [(i + 1, i) for i in range(seq_count - 1)]
    cores = [(0, 1), (1, 0)]

    spread = jnp.broadcast_to(w_out[None], (lax.axis_size("y"),) + w_out.shape)
    out_part = lax.all_to_all(spread, "y", 0, 0).reshape(-1, w_out.shape[1])
    out_part, w_in = lax.optimization_barrier((out_part, w_in))
    out_rows = lax.all_gather(out_part, "z", axis=0, tiled=True)
    in_part = lax.all_gather(w_in, "y", axis=0, tiled=True)
    in_rows = lax.all_gather(in_part, "z", axis=0, tiled=True)
    out_own = lax.all_gather(d_out, "x")
    out_other = lax.ppermute(out_own, "k", cores)
    prev = lax.ppermute(x_branch[tok_rows - 16 :], SEQ, forward)
    log_table = decay_table(tok_rows * seq_count)
    onehot = decay_level[:, None] == jnp.arange(LEVELS)[None, :]
    log_decay = jnp.sum(jnp.where(onehot, log_table[None, :], 0.0), axis=1)[None, :]
    decay, beta, conv_out, cum_decay, local_states, post, slope, ends, front_b = before(
        x_branch, prev, recurrence_gate, input_gate, conv_weight, conv_bias[None, :], log_decay
    )

    next_b = lax.ppermute(front_b, SEQ, backward)

    ends, next_b, in_part = lax.optimization_barrier((ends, next_b, in_part))
    d_lru, adj_local, offset, front_a, carry = adjoint(
        core, out_own, out_other, out_rows, gate_branch, decay, beta, input_gate, ends, seq_count
    )
    next_a = lax.ppermute(front_a, SEQ, backward)
    carries = lax.all_to_all(carry, SEQ, 0, 0)
    d_branch, kappa = branch(place, carries, offset, slope, conv_weight, next_a, next_b)
    own = lax.all_gather(d_branch, "x")
    other = lax.ppermute(own, "k", cores)
    d_gate, d_recurrence_gate, d_input_gate = gates(
        place, carries, kappa, d_lru, adj_local, post, cum_decay, local_states, decay,
        beta, conv_out, gate_branch, recurrence_gate, input_gate, log_decay,
    )
    d_input = input_grad(core, own, other, in_rows)
    return (d_input, d_gate, d_recurrence_gate, d_input_gate)


def solution(mesh):
    fine = Mesh(mesh.devices.reshape(8, 8, 4, 2), SEQ + CHAN)
    tokens = P(SEQ, CHAN)
    rows = P(CHAN + SEQ, None)
    in_specs = (tokens,) * 5 + (P(None, CHAN), P(CHAN), P(CHAN), rows, rows)
    return jax.shard_map(
        shards, mesh=fine, in_specs=in_specs, out_specs=(tokens,) * 4, check_vma=False
    )
```

```python
import functools

import jax
import jax.numpy as jnp
from jax import lax
from jax.experimental import pallas as pl
from jax.experimental.pallas import tpu as pltpu
from jax.sharding import Mesh, PartitionSpec as P

LEVELS = 16
SEQ = ("z", "y")
CHAN = ("x", "k")
SUB = 8
F32 = jnp.float32
BF16 = jnp.bfloat16
VMEM_LIMIT = 24 * 1024 * 1024
VMEM_WHOLE = 61 * 1024 * 1024


def decay_table(length):
    levels = jnp.arange(LEVELS).astype(F32)
    half = LEVELS // 2
    slow_rates = 0.25 * jnp.power(16.0, levels / (half - 1.0)) / (8.0 * length)
    fast_rates = jnp.power(4.0, (levels - half) / (half - 1.0)) / 640.0
    return -jnp.where(levels < half, slow_rates, fast_rates)


def gelu_parts(gate):
    normal_cdf = 0.5 * (1.0 + lax.erf(gate * 0.7071067811865476))
    density = jnp.exp(-0.5 * gate * gate) * 0.3989422804014327
    return (gate * normal_cdf, normal_cdf + gate * density)


def sigmoid(value):
    return 1.0 / (1.0 + jnp.exp(-value))


def expm1(value):
    series = jnp.ones_like(value)
    for term in range(9, 1, -1):
        series = 1.0 + value * (1.0 / term) * series
    return jnp.where(jnp.abs(value) < 0.5, value * series, jnp.exp(value) - 1.0)


def local_scan(a, b, reverse, a_out, b_out):
    rows, width = a.shape
    tiles = rows // SUB
    a = a.reshape(tiles, SUB, width)
    b = b.reshape(tiles, SUB, width)
    row = lax.broadcasted_iota(jnp.int32, a.shape, 1)
    for step in (1, 2, 4):
        shift = SUB - step if reverse else step
        inside = row < SUB - step if reverse else row >= step
        a_from = jnp.where(inside, pltpu.roll(a, shift, 1), 1.0)
        b_from = jnp.where(inside, pltpu.roll(b, shift, 1), 0.0)
        b = b + a * b_from
        a = a * a_from
    prod = jnp.ones((1, width), F32)
    state = jnp.zeros((1, width), F32)
    edge = 0 if reverse else SUB - 1
    for tile in reversed(range(tiles)) if reverse else range(tiles):
        here_b = b[tile] + a[tile] * state
        here_a = a[tile] * prod
        b_out[pl.ds(tile * SUB, SUB), :] = here_b
        a_out[pl.ds(tile * SUB, SUB), :] = here_a
        state = here_b[edge : edge + 1]
        prod = here_a[edge : edge + 1]
    return prod, state


def shift_up(value, last):
    rows = value.shape[0]
    row = lax.broadcasted_iota(jnp.int32, value.shape, 0)
    return jnp.where(row == rows - 1, last, pltpu.roll(value, rows - 1, 0))


def before_kernel(
    x_ref, prev_ref, rec_ref, inw_ref, cw_ref, cb_ref, ld_ref,
    decay_ref, beta_ref, conv_ref, cum_ref, local_ref, post_ref, slope_ref, ends_ref, front_ref,
    padded, scan_a, scan_b,
):
    rows = x_ref.shape[0]
    lead = prev_ref.shape[0]
    padded[pl.ds(0, lead), :] = prev_ref[...].astype(F32)
    padded[pl.ds(lead, rows), :] = x_ref[...].astype(F32)
    conv = jnp.zeros(x_ref.shape, F32)
    for lag in range(4):
        conv = conv + cw_ref[lag : lag + 1, :] * padded[pl.ds(lead - lag, rows), :]
    conv = cb_ref[...] + conv
    recur = sigmoid(rec_ref[...].astype(F32))
    inward = sigmoid(inw_ref[...].astype(F32))
    log_step = 8.0 * recur * ld_ref[...]
    decay = jnp.exp(log_step)
    beta = jnp.sqrt(-expm1(2.0 * log_step))
    decay_ref[...] = decay
    beta_ref[...] = beta
    conv_ref[...] = conv
    prod, state = local_scan(decay, beta * (inward * conv), False, cum_ref, local_ref)
    ends_ref[...] = jnp.concatenate([prod, state], axis=0)
    local_scan(decay, jnp.zeros_like(decay), True, scan_a, scan_b)
    post = shift_up(scan_a[...], 1.0)
    post_ref[...] = post
    slope = post * beta * inward
    slope_ref[...] = slope
    front_ref[...] = slope[:SUB]


def before(
    x_branch, prev, recurrence_gate, input_gate, conv_weight, conv_bias, log_decay
):
    rows, width = x_branch.shape
    full = jax.ShapeDtypeStruct((rows, width), F32)
    return pl.pallas_call(
        before_kernel,
        out_shape=(full,) * 7
        + (
            jax.ShapeDtypeStruct((2, width), F32),
            jax.ShapeDtypeStruct((SUB, width), F32),
        ),
        scratch_shapes=[
            pltpu.VMEM((rows + prev.shape[0], width), F32),
            pltpu.VMEM((rows, width), F32),
            pltpu.VMEM((rows, width), F32),
        ],
        compiler_params=pltpu.CompilerParams(vmem_limit_bytes=VMEM_LIMIT),
    )(x_branch, prev, recurrence_gate, input_gate, conv_weight, conv_bias, log_decay)


def adjoint_kernel(
    core_ref, own_ref, other_ref, w_ref, gate_ref, decay_ref, beta_ref, inw_ref, ends_ref,
    dlru_ref, adj_ref, offset_ref, front_ref, carry_ref,
    acc, scan_a, scan_b,
):
    step = pl.program_id(0)
    half = w_ref.shape[1] // 2

    @pl.when(step == 0)
    def _():
        acc[...] = jnp.zeros_like(acc)

    def add(first, second):
        dims = (((1,), (1,)), ((), ()))
        acc[...] += lax.dot_general(
            first, w_ref[:, :half], dims, preferred_element_type=F32
        ) + lax.dot_general(second, w_ref[:, half:], dims, preferred_element_type=F32)

    @pl.when(core_ref[0] == 0)
    def _():
        add(own_ref[0], other_ref[0])

    @pl.when(core_ref[0] != 0)
    def _():
        add(other_ref[0], own_ref[0])

    @pl.when(step == pl.num_programs(0) - 1)
    def _():
        d_lru = acc[...]
        dlru_ref[...] = d_lru
        d_direct = d_lru * gelu_parts(gate_ref[...].astype(F32))[0]
        decay = decay_ref[...]
        _, first = local_scan(decay, decay * d_direct, True, scan_a, scan_b)
        adj = d_direct + shift_up(scan_b[...], 0.0)
        adj_ref[...] = adj
        offset = adj * beta_ref[...] * sigmoid(inw_ref[...].astype(F32))
        offset_ref[...] = offset
        front_ref[...] = offset[:SUB]
        mine = jnp.concatenate([ends_ref[...], first], axis=0)
        carry_ref[...] = jnp.broadcast_to(mine[None], carry_ref.shape)


def adjoint(core, own, other, weights, gate, decay, beta, input_gate, ends, seq_count):
    rows, width = gate.shape
    steps = own.shape[0]
    full = jax.ShapeDtypeStruct((rows, width), F32)
    whole = lambda shape: pl.BlockSpec(shape, lambda i: (0,) * len(shape))
    return pl.pallas_call(
        adjoint_kernel,
        grid=(steps,),
        in_specs=[
            pl.BlockSpec(memory_space=pltpu.SMEM),
            pl.BlockSpec((1, rows, width), lambda i: (i, 0, 0)),
            pl.BlockSpec((1, rows, width), lambda i: (i, 0, 0)),
            pl.BlockSpec((width, 2 * width), lambda i: (0, i)),
            whole((rows, width)),
            whole((rows, width)),
            whole((rows, width)),
            whole((rows, width)),
            whole((2, width)),
        ],
        out_specs=[
            whole((rows, width)),
            whole((rows, width)),
            whole((rows, width)),
            whole((SUB, width)),
            whole((seq_count, 3, width)),
        ],
        out_shape=(
            full,
            full,
            full,
            jax.ShapeDtypeStruct((SUB, width), F32),
            jax.ShapeDtypeStruct((seq_count, 3, width), F32),
        ),
        scratch_shapes=[pltpu.VMEM((rows, width), F32)] * 3,
        compiler_params=pltpu.CompilerParams(vmem_limit_bytes=VMEM_WHOLE),
    )(core, own, other, weights, gate, decay, beta, input_gate, ends)


def branch_kernel(
    place_ref, carry_ref, offset_ref, slope_ref, cw_ref, front_a_ref, front_b_ref,
    branch_ref, kappa_ref,
    padded,
):
    rows, width = offset_ref.shape
    place = place_ref[0]
    beyond = jnp.zeros((1, width), F32)
    kappa = jnp.zeros((1, width), F32)
    for i in reversed(range(1, carry_ref.shape[0])):
        here = carry_ref[i, 2:3] + carry_ref[i, 0:1] * kappa
        beyond = jnp.where(i == place + 1, kappa, beyond)
        kappa = jnp.where(i > place, here, kappa)
    padded[pl.ds(0, rows), :] = offset_ref[...] + slope_ref[...] * kappa
    padded[pl.ds(rows, SUB), :] = front_a_ref[...] + front_b_ref[...] * beyond
    total = jnp.zeros((rows, width), F32)
    for lag in range(4):
        total = total + cw_ref[lag : lag + 1, :] * padded[pl.ds(lag, rows), :]
    branch_ref[...] = total.astype(BF16)
    kappa_ref[...] = kappa


def branch(place, carry, offset, slope, conv_weight, front_a, front_b):
    rows, width = offset.shape
    vmem = pl.BlockSpec(memory_space=pltpu.VMEM)
    return pl.pallas_call(
        branch_kernel,
        in_specs=[pl.BlockSpec(memory_space=pltpu.SMEM)] + [vmem] * 6,
        out_shape=(
            jax.ShapeDtypeStruct((rows, width), BF16),
            jax.ShapeDtypeStruct((1, width), F32),
        ),
        scratch_shapes=[pltpu.VMEM((rows + SUB, width), F32)],
        compiler_params=pltpu.CompilerParams(vmem_limit_bytes=VMEM_LIMIT),
    )(place, carry, offset, slope, conv_weight, front_a, front_b)


def gates_kernel(
    place_ref, carry_ref, kappa_ref, dlru_ref, adj_ref, post_ref, cum_ref, local_ref, decay_ref,
    beta_ref, conv_ref, gate_ref, rec_ref, inw_ref, ld_ref,
    dgate_ref, drec_ref, dinw_ref,
):
    place = place_ref[0]
    carried = jnp.zeros(kappa_ref.shape, F32)
    for i in range(carry_ref.shape[0] - 1):
        carried = jnp.where(i < place, carry_ref[i, 1:2] + carry_ref[i, 0:1] * carried, carried)
    states = local_ref[...] + cum_ref[...] * carried
    slope = gelu_parts(gate_ref[...].astype(F32))[1]
    dgate_ref[...] = (dlru_ref[...].astype(F32) * states * slope).astype(BF16)
    row = lax.broadcasted_iota(jnp.int32, states.shape, 0)
    states_prev = jnp.where(row == 0, carried, pltpu.roll(states, 1, 0))
    recur = sigmoid(rec_ref[...].astype(F32))
    inward = sigmoid(inw_ref[...].astype(F32))
    decay = decay_ref[...]
    beta = beta_ref[...]
    conv = conv_ref[...]
    adj = adj_ref[...] + post_ref[...] * kappa_ref[...]
    d_step = adj * (decay * states_prev - inward * conv * decay * decay / beta)
    drec_ref[...] = (d_step * 8.0 * ld_ref[...] * recur * (1.0 - recur)).astype(BF16)
    dinw_ref[...] = (adj * beta * conv * inward * (1.0 - inward)).astype(BF16)


def gates(place, carry, kappa, d_lru, *arrays):
    out = jax.ShapeDtypeStruct(d_lru.shape, BF16)
    vmem = pl.BlockSpec(memory_space=pltpu.VMEM)
    return pl.pallas_call(
        gates_kernel,
        in_specs=[pl.BlockSpec(memory_space=pltpu.SMEM)] + [vmem] * (3 + len(arrays)),
        out_shape=(out,) * 3,
        compiler_params=pltpu.CompilerParams(vmem_limit_bytes=VMEM_LIMIT),
    )(place, carry, kappa, d_lru, *arrays)


def input_kernel(lead, core_ref, blocks_ref, first_ref, rest_ref, start_ref, out_ref, acc):
    step = pl.program_id(0)
    half = first_ref.shape[1] // 2

    @pl.when(step == 0)
    def _():
        acc[...] = start_ref[...]

    def add(w_ref, at):
        acc[...] += lax.dot_general(
            blocks_ref[0], w_ref[:, at : at + half], (((1,), (1,)), ((), ())),
            preferred_element_type=F32,
        )

    for core, at in ((0, 0), (1, half)):

        @pl.when((core_ref[0] == core) & (step < lead))
        def _():
            add(first_ref, at)

        @pl.when((core_ref[0] == core) & (step >= lead))
        def _():
            add(rest_ref, at)

    @pl.when(step == pl.num_programs(0) - 1)
    def _():
        out_ref[...] = acc[...].astype(out_ref.dtype)


def input_grad(core, blocks, first, rest, start, dtype):
    steps, rows, width = blocks.shape
    feats = first.shape[0]
    lead = steps - rest.shape[1] // (2 * width)
    at = first.shape[1] // (2 * width) - lead
    return pl.pallas_call(
        functools.partial(input_kernel, lead),
        grid=(steps,),
        in_specs=[
            pl.BlockSpec(memory_space=pltpu.SMEM),
            pl.BlockSpec((1, rows, width), lambda i: (i, 0, 0)),
            pl.BlockSpec((feats, 2 * width), lambda i: (0, at + jnp.minimum(i, lead - 1))),
            pl.BlockSpec((feats, 2 * width), lambda i: (0, jnp.maximum(i - lead, 0))),
            pl.BlockSpec((rows, feats), lambda i: (0, 0)),
        ],
        out_specs=pl.BlockSpec((rows, feats), lambda i: (0, 0)),
        out_shape=jax.ShapeDtypeStruct((rows, feats), dtype),
        scratch_shapes=[pltpu.VMEM((rows, feats), F32)],
        compiler_params=pltpu.CompilerParams(vmem_limit_bytes=VMEM_WHOLE),
    )(core, blocks, first, rest, start)


def shards(
    d_out,
    x_branch,
    gate_branch,
    recurrence_gate,
    input_gate,
    conv_weight,
    conv_bias,
    decay_level,
    w_in,
    w_out,
):
    tok_rows, width = x_branch.shape
    seq_count = lax.axis_size(SEQ)
    place = lax.axis_index(SEQ).astype(jnp.int32).reshape(1)
    core = lax.axis_index("k").astype(jnp.int32).reshape(1)
    forward = [(i, i + 1) for i in range(seq_count - 1)]
    backward = [(i + 1, i) for i in range(seq_count - 1)]
    cores = [(0, 1), (1, 0)]

    half = w_in.shape[1] // 2
    first = jnp.concatenate([w_out, w_in[:, :half]], axis=1)
    first = lax.all_gather(first, SEQ, axis=0, tiled=True)
    rest = lax.all_gather(w_in[:, half:], "y", axis=0, tiled=True)
    in_rows = lax.all_gather(rest, "z", axis=0, tiled=True)
    out_own = lax.all_gather(d_out, "x")
    out_other = lax.ppermute(out_own, "k", cores)
    prev = lax.ppermute(x_branch[tok_rows - 16 :], SEQ, forward)
    log_table = decay_table(tok_rows * seq_count)
    onehot = decay_level[:, None] == jnp.arange(LEVELS)[None, :]
    log_decay = jnp.sum(jnp.where(onehot, log_table[None, :], 0.0), axis=1)[None, :]
    decay, beta, conv_out, cum_decay, local_states, post, slope, ends, front_b = before(
        x_branch, prev, recurrence_gate, input_gate, conv_weight, conv_bias[None, :], log_decay
    )

    next_b = lax.ppermute(front_b, SEQ, backward)

    ends, next_b = lax.optimization_barrier((ends, next_b))
    d_lru, adj_local, offset, front_a, carry = adjoint(
        core, out_own, out_other, first, gate_branch, decay, beta, input_gate, ends, seq_count
    )
    next_a = lax.ppermute(front_a, SEQ, backward)
    carries = lax.all_to_all(carry, SEQ, 0, 0)
    d_branch, kappa = branch(place, carries, offset, slope, conv_weight, next_a, next_b)
    own = lax.all_gather(d_branch, "x")
    other = lax.ppermute(own, "k", cores)
    d_gate, d_recurrence_gate, d_input_gate = gates(
        place, carries, kappa, d_lru, adj_local, post, cum_decay, local_states, decay,
        beta, conv_out, gate_branch, recurrence_gate, input_gate, log_decay,
    )
    start = jnp.zeros((tok_rows, first.shape[0]), F32)
    start = input_grad(core, own, first, in_rows, start, F32)
    d_input = input_grad(1 - core, other, first, in_rows, start, BF16)
    return (d_input, d_gate, d_recurrence_gate, d_input_gate)


def solution(mesh):
    fine = Mesh(mesh.devices.reshape(8, 8, 4, 2), SEQ + CHAN)
    tokens = P(SEQ, CHAN)
    rows = P(CHAN + SEQ, None)
    in_specs = (tokens,) * 5 + (P(None, CHAN), P(CHAN), P(CHAN), rows, rows)
    return jax.shard_map(
        shards, mesh=fine, in_specs=in_specs, out_specs=(tokens,) * 4, check_vma=False
    )
```
